256 devices in a mesh: prompt: 16 (over z_lo, y), roll: 16 (over z_hi, x, core).
Axes of the slice: x: 4, y: 4, z: 8 (z_hi: 2, z_lo: 4; z = z_hi * 4 + z_lo), core: 2. Of those that a mesh axis runs over, the one named last changes fastest.
Arguments:
- pre_q: bfloat16 [16384, 1024], P(('prompt', 'roll')), parts along dimension 0, may hold values from -8 to 8
- pre_kv: bfloat16 [16384, 256], P(('prompt', 'roll')), parts along dimension 0, may hold values from -8 to 8
- roll_q: bfloat16 [256, 128, 1024], P(('prompt', 'roll')), parts along dimension 0, may hold values from -8 to 8
- roll_kv: bfloat16 [256, 128, 256], P(('prompt', 'roll')), parts along dimension 0, may hold values from -8 to 8
- pre_grad: bfloat16 [16384, 1024], P(('prompt', 'roll')), parts along dimension 0, may hold values from -6 to 6
- roll_grad: bfloat16 [256, 128, 1024], P(('prompt', 'roll')), parts along dimension 0, may hold values from -6 to 6
- pre_len: int32 [16], P('prompt'), parts along dimension 0, may hold values from 512 to 1024, as said below
- roll_len: int32 [256], P(('prompt', 'roll')), parts along dimension 0, may hold values from 32 to 128, as said below
Outputs:
- pre_out: bfloat16 [16384, 1024], P(('prompt', 'roll')), parts along dimension 0
- roll_out: bfloat16 [256, 128, 1024], P(('prompt', 'roll')), parts along dimension 0
- pre_dq: bfloat16 [16384, 1024], P(('prompt', 'roll')), parts along dimension 0
- roll_dq: bfloat16 [256, 128, 1024], P(('prompt', 'roll')), parts along dimension 0
- pre_dkv: bfloat16 [16384, 256], P(('prompt', 'roll')), parts along dimension 0
- roll_dkv: bfloat16 [256, 128, 256], P(('prompt', 'roll')), parts along dimension 0
The draws below stay inside these ranges and needn't reach their ends.
There are 16 independent parts, one for each index of `prompt`. The reference program is written for one: setup_inputs(seed, part) draws one part's arguments, and reference() takes and returns one part's arrays. A program takes and returns all parts, laid end to end along the dimension named above; each array names one. Nothing has to cross between parts.
Inputs may be any that keep to these rules, and one draw needn't show every extreme that they name: `pre_len`: valid prefix positions of the prompt; later positions are padding. `roll_len`: valid tokens of each rollout; later tokens are padding; one rollout of each prompt has 128.
All inputs are finite; a program needn't handle non-finite values.
Results may differ from the reference program's by a relative error of at most 0.03.
Values may be sent and summed in bfloat16 or wider, within the bound.
A program may use at most 64 MiB of HBM per device.

```python
import jax
import jax.numpy as jnp
from jax import lax

HEADS = 8
HD = 128
RESP = 128
PREFIX = 1024
ROLLOUTS = 16


def draw_pre_q(key, part):
    key = jax.random.fold_in(key, 11)
    sample = jnp.clip(1.5 * jax.random.normal(key, (PREFIX, HEADS, HD), jnp.float32), -6.0, 6.0)
    return sample.reshape(PREFIX, HEADS * HD).astype(jnp.bfloat16)


def draw_roll_q(key, part):
    key = jax.random.fold_in(key, 12)
    sample = jnp.clip(1.5 * jax.random.normal(key, (ROLLOUTS, RESP, HEADS, HD), jnp.float32), -6.0, 6.0)
    return sample.reshape(ROLLOUTS, RESP, HEADS * HD).astype(jnp.bfloat16)


def draw_pre_kv(key, part):
    key = jax.random.fold_in(key, 13)
    key_part, val_part = jax.random.split(key)
    key_rows = jnp.clip(jax.random.normal(key_part, (PREFIX, HD), jnp.float32), -6.0, 6.0)
    val_rows = jnp.clip(3.0 * jax.random.normal(val_part, (PREFIX, HD), jnp.float32), -8.0, 8.0)
    return jnp.concatenate([key_rows, val_rows], axis=1).astype(jnp.bfloat16)


def draw_roll_kv(key, part):
    key = jax.random.fold_in(key, 17)
    key_part, val_part = jax.random.split(key)
    key_rows = jnp.clip(jax.random.normal(key_part, (ROLLOUTS, RESP, HD), jnp.float32), -6.0, 6.0)
    val_rows = jnp.clip(3.0 * jax.random.normal(val_part, (ROLLOUTS, RESP, HD), jnp.float32), -8.0, 8.0)
    return jnp.concatenate([key_rows, val_rows], axis=2).astype(jnp.bfloat16)


def draw_pre_len(key, part):
    key = jax.random.fold_in(key, 19)
    drawn = jax.random.randint(key, (1,), PREFIX // 2, PREFIX + 1, dtype=jnp.int32)
    return jnp.where(part % 2 == 1, PREFIX, drawn).astype(jnp.int32)


def draw_roll_len(key, part):
    key = jax.random.fold_in(key, 23)
    len_key, pick_key = jax.random.split(key)
    lengths = jax.random.randint(len_key, (ROLLOUTS,), RESP // 4, RESP + 1, dtype=jnp.int32)
    longest = jax.random.randint(pick_key, (), 0, ROLLOUTS, dtype=jnp.int32)
    return jnp.where(jnp.arange(ROLLOUTS, dtype=jnp.int32) == longest, RESP, lengths).astype(jnp.int32)


def level_of(own_key, extent, cuts, smallest, top_value):
    loudness, own = 1.0, jax.random.fold_in(own_key, 6)
    for axis_at, shards_of in cuts:
        steps = jnp.exp(jax.random.uniform(jax.random.fold_in(own, axis_at), (shards_of,), jnp.float32, smallest / len(cuts), top_value / len(cuts)))
        loudness = loudness * jnp.repeat(steps, extent[axis_at] // shards_of).reshape([-1 if axis == axis_at else 1 for axis in range(len(extent))])
    return loudness


def scatter_about(key, dims, deviation, most, cuts=(), kind=jnp.bfloat16):
    result = jax.random.normal(key, dims, jnp.float32) * deviation
    if len(cuts) > 0:
        result = level_of(key, dims, cuts, -0.22, 0.18) * result
    return jnp.clip(result, min=-most, max=most).astype(kind)


def setup_inputs(seed: int = 0, part: int = 0) -> dict:
    splits = jax.random.split(jax.random.key(seed), 9)
    part_keys = jax.random.split(jax.random.fold_in(splits[8], part), 9)
    pre_q = draw_pre_q(jax.random.fold_in(jax.random.fold_in(splits[8], part), 71), part)
    pre_kv = draw_pre_kv(jax.random.fold_in(jax.random.fold_in(splits[8], part), 71), part)
    roll_q = draw_roll_q(jax.random.fold_in(jax.random.fold_in(splits[8], part), 71), part)
    roll_kv = draw_roll_kv(jax.random.fold_in(jax.random.fold_in(splits[8], part), 71), part)
    pre_grad = scatter_about(part_keys[4], (PREFIX, HEADS * HD), 1.0, 6.0, ((0, 16),))
    roll_grad = scatter_about(part_keys[5], (ROLLOUTS, RESP, HEADS * HD), 1.0, 6.0, ((0, 16),))
    pre_len = draw_pre_len(jax.random.fold_in(jax.random.fold_in(splits[8], part), 71), part)
    roll_len = draw_roll_len(jax.random.fold_in(jax.random.fold_in(splits[8], part), 71), part)
    return dict(pre_q=pre_q, pre_kv=pre_kv, roll_q=roll_q, roll_kv=roll_kv, pre_grad=pre_grad, roll_grad=roll_grad, pre_len=pre_len, roll_len=roll_len)


masked_score = -1e30


def rounded(values):
    return lax.optimization_barrier(values.astype(jnp.bfloat16)).astype(jnp.float32)


def attend(query, grads, key_rows, val_rows, allowed, live_rows):
    score_scale = HD ** -0.5
    query_f = query.astype(jnp.float32)
    key_f = key_rows.astype(jnp.float32)
    val_f = val_rows.astype(jnp.float32)
    grad_f = jnp.where(live_rows[:, None, None], grads, jnp.zeros_like(grads)).astype(jnp.float32)
    logits = jnp.einsum('rhd,kd->hrk', query_f, key_f) * score_scale
    row_max = jnp.max(jnp.where(allowed[None], logits, masked_score), axis=-1)
    expo = jnp.where(allowed[None], jnp.exp(logits - row_max[..., None]), 0.0)
    row_sum = jnp.sum(expo, axis=-1)
    output = jnp.einsum('hrk,kd->hrd', rounded(expo), val_f) / row_sum[..., None]
    output = jnp.where(live_rows[:, None, None], output.transpose(1, 0, 2), 0.0).astype(jnp.bfloat16)
    out_f = output.astype(jnp.float32)
    row_dot = jnp.sum(grad_f * out_f, axis=-1).T
    log_total = row_max + jnp.log(row_sum)
    probs = jnp.where(allowed[None], jnp.exp(logits - log_total[..., None]), 0.0)
    grad_probs = jnp.einsum('rhd,kd->hrk', grad_f, val_f)
    grad_logits = probs * (grad_probs - row_dot[..., None])
    grad_vals = jnp.einsum('hrk,rhd->kd', rounded(probs), grad_f)
    grad_keys = jnp.einsum('hrk,rhd->kd', rounded(grad_logits), query_f) * score_scale
    grad_query = jnp.einsum('hrk,kd->rhd', rounded(grad_logits), key_f) * score_scale
    return output, grad_query, grad_keys, grad_vals


def reference(pre_q, pre_kv, roll_q, roll_kv, pre_grad, roll_grad, pre_len, roll_len):
    prefix_len = pre_len[0]
    key_pos = jnp.arange(PREFIX, dtype=jnp.int32)
    pre_keys = pre_kv[:, :HD]
    pre_vals = pre_kv[:, HD:]
    block_rows = min(256, PREFIX)
    block_count = PREFIX // block_rows

    def prefix_block(index):
        first = index * block_rows
        query = lax.dynamic_slice_in_dim(pre_q, first, block_rows, 0).reshape(block_rows, HEADS, HD)
        grads = lax.dynamic_slice_in_dim(pre_grad, first, block_rows, 0).reshape(block_rows, HEADS, HD)
        query_pos = first + jnp.arange(block_rows, dtype=jnp.int32)
        allowed = (key_pos[None, :] <= query_pos[:, None]) & (key_pos < prefix_len)[None, :]
        return attend(query, grads, pre_keys, pre_vals, allowed, query_pos < prefix_len)

    p_out, p_dq, p_dk, p_dv = lax.map(prefix_block, jnp.arange(block_count, dtype=jnp.int32))
    resp_pos = jnp.arange(RESP, dtype=jnp.int32)

    def rollout(pieces):
        query, grads, kv_rows, length = pieces
        key_rows = jnp.concatenate([pre_keys, kv_rows[:, :HD]], axis=0)
        val_rows = jnp.concatenate([pre_vals, kv_rows[:, HD:]], axis=0)
        own_ok = (resp_pos[None, :] <= resp_pos[:, None]) & (resp_pos < length)[None, :]
        prefix_ok = jnp.broadcast_to((key_pos < prefix_len)[None, :], (RESP, PREFIX))
        allowed = jnp.concatenate([prefix_ok, own_ok], axis=1)
        return attend(query.reshape(RESP, HEADS, HD), grads.reshape(RESP, HEADS, HD), key_rows, val_rows, allowed, resp_pos < length)

    r_out, r_dq, r_dk, r_dv = lax.map(rollout, (roll_q, roll_grad, roll_kv, roll_len))
    pre_dk = jnp.sum(p_dk, axis=0) + jnp.sum(r_dk[:, :PREFIX], axis=0)
    pre_dv = jnp.sum(p_dv, axis=0) + jnp.sum(r_dv[:, :PREFIX], axis=0)
    pre_out = p_out.reshape(PREFIX, HEADS * HD)
    pre_dq = p_dq.reshape(PREFIX, HEADS * HD).astype(jnp.bfloat16)
    roll_out = r_out.reshape(ROLLOUTS, RESP, HEADS * HD)
    roll_dq = r_dq.reshape(ROLLOUTS, RESP, HEADS * HD).astype(jnp.bfloat16)
    pre_dkv = jnp.concatenate([pre_dk, pre_dv], axis=1).astype(jnp.bfloat16)
    roll_dkv = jnp.concatenate([r_dk[:, PREFIX:], r_dv[:, PREFIX:]], axis=2).astype(jnp.bfloat16)
    return (pre_out, roll_out, pre_dq, roll_dq, pre_dkv, roll_dkv)
```

```python
import functools

import jax
import jax.numpy as jnp
from jax import lax
from jax.experimental import pallas as pl
from jax.experimental.pallas import tpu as pltpu
from jax.sharding import PartitionSpec as P

F32 = jnp.float32
BF16 = jnp.bfloat16
MESH = pl.DeviceIdType.MESH
masked_score = -1e30
HALVES, ROW, CORES = 2, 4, 2
BLOCK = 64
RESP = 128
HEADS = 8
HD = 128
GROUP = HALVES * ROW * CORES
CHUNK = ROW * BLOCK
PREFIX = GROUP * BLOCK
ROLL_ROWS = HEADS * RESP
ROWS = HEADS * (RESP + BLOCK)
SCALE = HD**-0.5
LOG2E = 1.4426950408889634


def dot(left, right, left_dim, right_dim):
    return lax.dot_general(
        left, right, (((left_dim,), (right_dim,)), ((), ())), preferred_element_type=F32
    )


def slot(half, core, place):
    return (half * CORES + core) * ROW + place


def block_of(half, core, place):
    return pl.ds(slot(half, core, place) * BLOCK, BLOCK)


def chunk_of(half, core):
    return pl.ds((half * CORES + core) * CHUNK, CHUNK)


def fold8(values, combine):
    return combine(values.reshape(values.shape[0] // 8, 8, values.shape[1]), axis=0)


def kernel(
    pre_len_ref,
    roll_len_ref,
    pre_q,
    pre_kv,
    roll_q,
    roll_kv,
    pre_grad,
    roll_grad,
    pre_out,
    roll_out,
    pre_dq,
    roll_dq,
    pre_dkv,
    roll_dkv,
    rq,
    rg,
    pq,
    pg,
    rkv,
    kvs,
    queries,
    grads,
    score,
    weight,
    gradp,
    keys_t,
    vals_t,
    to_core,
    from_core,
    own_sum,
    to_row,
    from_row,
    to_half,
    from_half,
    load_sem,
    send_sem,
    recv_sem,
    sum_send_sem,
    sum_recv_sem,
):
    me = lax.axis_index("roll")
    my_half, my_place, my_core = me // (ROW * CORES), (me // CORES) % ROW, me % CORES

    def device(half, core, place):
        return (
            ((my_half + half) % HALVES) * (ROW * CORES)
            + ((my_place + place) % ROW) * CORES
            + (my_core + core) % CORES
        )

    partners = [(1, 0, 0), (0, 1, 0), (0, 0, 1), (0, 0, 3), (0, 0, 2)]
    barrier = pltpu.get_barrier_semaphore()
    for partner in partners:
        pl.semaphore_signal(
            barrier, inc=1, device_id={"roll": device(*partner)}, device_id_type=MESH
        )

    loads = []
    for index, (source, target) in enumerate(
        (
            (pre_kv, kvs.at[block_of(0, 0, 0)]),
            (roll_kv.at[0], rkv),
            (roll_q.at[0], rq),
            (pre_q, pq),
            (roll_grad.at[0], rg),
            (pre_grad, pg),
        )
    ):
        loads.append(pltpu.make_async_copy(source, target, load_sem.at[index]))
        loads[-1].start()

    def push(source, half, core, place, to):
        at = slot(half, core, place)
        copy = pltpu.make_async_remote_copy(
            src_ref=source,
            dst_ref=kvs.at[block_of(half, core, place)],
            send_sem=send_sem.at[at],
            recv_sem=recv_sem.at[at],
            device_id={"roll": device(*to)},
            device_id_type=MESH,
        )
        copy.start()
        return copy

    pl.semaphore_wait(barrier, len(partners))
    copies = {}
    copies[1, 0, 0] = push(pre_kv, 1, 0, 0, (1, 0, 0))
    for place in (1, 3, 2):
        copies[0, 0, ROW - place] = push(pre_kv, 0, 0, ROW - place, (0, 0, place))
    copies[0, 1, 0] = push(pre_kv, 0, 1, 0, (0, 1, 0))

    pre_len = pre_len_ref[0]
    roll_len = roll_len_ref[0]
    lane = lax.broadcasted_iota(jnp.int32, (1, ROWS), 1)
    is_roll = lane < ROLL_ROWS
    query_pos = me * BLOCK + lane % BLOCK
    limit = jnp.where(is_roll, pre_len - 1, jnp.minimum(query_pos, pre_len - 1))
    own_limit = jnp.minimum(lane[:, :ROLL_ROWS] % RESP, roll_len - 1)
    rows_left = jnp.where(is_roll, roll_len - lane % RESP, pre_len - query_pos)

    for load in loads:
        load.wait()
    roll_live = lax.broadcasted_iota(jnp.int32, (RESP, HD), 0) < roll_len
    pre_live = lax.broadcasted_iota(jnp.int32, (BLOCK, HD), 0) + me * BLOCK < pre_len
    none = jnp.zeros((), BF16)
    for head in range(HEADS):
        columns = slice(head * HD, (head + 1) * HD)
        at = pl.ds(head * RESP, RESP)
        queries[at, :] = rq[:, columns]
        grads[at, :] = jnp.where(roll_live, rg[:, columns], none)
        at = pl.ds(ROLL_ROWS + head * BLOCK, BLOCK)
        queries[at, :] = pq[:, columns]
        grads[at, :] = jnp.where(pre_live, pg[:, columns], none)

    own_rows = pl.ds(PREFIX, RESP)
    own_cols = slice(0, ROLL_ROWS)

    def transpose_in(half, core):
        at = chunk_of(half, core)
        keys_t[:, at] = kvs[at, 0:HD].T
        vals_t[:, at] = kvs[at, HD : 2 * HD].T

    def scores_of(half, core):
        at = chunk_of(half, core)
        row = lax.broadcasted_iota(jnp.int32, (CHUNK, 1), 0)
        owner = (
            ((my_half + half) % HALVES) * (ROW * CORES)
            + ((my_place + row // BLOCK) % ROW) * CORES
            + (my_core + core) % CORES
        )
        key_pos = owner * BLOCK + row % BLOCK
        logits = dot(kvs[at, 0:HD], queries[...], 1, 1) * (SCALE * LOG2E)
        logits = jnp.where(key_pos <= limit, logits, masked_score)
        score[at, :] = logits
        return fold8(logits, jnp.max)

    def widen(total, own, combine):
        return jnp.concatenate([combine(total[:, own_cols], own), total[:, ROLL_ROWS:]], axis=1)

    def expo_of(half, core, row_max):
        at = chunk_of(half, core)
        expo = jnp.exp2(score[at, :] - row_max)
        rounded = expo.astype(BF16)
        weight[at, :] = rounded
        return fold8(expo, jnp.sum), dot(vals_t[:, at], rounded, 1, 0)

    own_key = lax.broadcasted_iota(jnp.int32, (RESP, 1), 0)
    own_logits = dot(rkv[:, 0:HD], queries[own_cols, :], 1, 1) * (SCALE * LOG2E)
    own_logits = jnp.where(own_key <= own_limit, own_logits, masked_score)
    score[own_rows, own_cols] = own_logits
    own_max = fold8(own_logits, jnp.max)
    keys_t[:, own_rows] = rkv[:, 0:HD].T
    vals_t[:, own_rows] = rkv[:, HD : 2 * HD].T
    gradp[own_rows, own_cols] = dot(rkv[:, HD : 2 * HD], grads[own_cols, :], 1, 1)
    grad_t = grads[...].T.astype(F32)

    for place in (1, 3, 2):
        copies[0, 0, place].wait_recv()
        copies[0, 1, place] = push(
            kvs.at[block_of(0, 0, place)], 0, 1, place, (0, 1, 0)
        )
    transpose_in(0, 0)
    near_max = scores_of(0, 0)
    copies[1, 0, 0].wait_recv()
    for place in (1, 3, 2):
        copies[1, 0, ROW - place] = push(
            kvs.at[block_of(1, 0, 0)], 1, 0, ROW - place, (0, 0, place)
        )
    copies[1, 1, 0] = push(kvs.at[block_of(1, 0, 0)], 1, 1, 0, (0, 1, 0))
    for place in range(ROW):
        copies[0, 1, place].wait_recv()
    transpose_in(0, 1)
    near_max = jnp.maximum(near_max, scores_of(0, 1))
    near_max = widen(near_max, own_max, jnp.maximum)
    near_max = jnp.max(near_max, axis=0, keepdims=True)
    for place in (1, 3, 2):
        copies[1, 0, place].wait_recv()
        copies[1, 1, place] = push(
            kvs.at[block_of(1, 0, place)], 1, 1, place, (0, 1, 0)
        )
    near_sum, near_out = expo_of(0, 0, near_max)
    more_sum, more_out = expo_of(0, 1, near_max)
    near_sum, near_out = near_sum + more_sum, near_out + more_out
    expo = jnp.exp2(score[own_rows, own_cols] - near_max[:, own_cols])
    rounded = expo.astype(BF16)
    weight[own_rows, own_cols] = rounded
    near_sum = widen(near_sum, fold8(expo, jnp.sum), jnp.add)
    near_out = widen(near_out, dot(vals_t[:, own_rows], rounded, 1, 0), jnp.add)
    near_sum = jnp.sum(near_sum, axis=0, keepdims=True)
    for core in range(CORES):
        at = chunk_of(0, core)
        gradp[at, :] = dot(kvs[at, HD : 2 * HD], grads[...], 1, 1)

    transpose_in(1, 0)
    far_max = scores_of(1, 0)
    for place in range(ROW):
        copies[1, 1, place].wait_recv()
    transpose_in(1, 1)
    far_max = jnp.maximum(far_max, scores_of(1, 1))
    far_max = jnp.max(far_max, axis=0, keepdims=True)
    row_max = jnp.maximum(near_max, far_max)
    shrink = jnp.exp2(near_max - row_max)
    far_sum, far_out = expo_of(1, 0, row_max)
    more_sum, more_out = expo_of(1, 1, row_max)
    far_sum = jnp.sum(far_sum + more_sum, axis=0, keepdims=True)
    row_sum = near_sum * shrink + far_sum
    inverse = 1.0 / row_sum
    out_t = near_out * shrink + (far_out + more_out)
    out_t = (out_t * jnp.where(rows_left > 0, inverse, 0.0)).astype(BF16)
    row_dot = jnp.sum(grad_t * out_t.astype(F32), axis=0, keepdims=True)
    factors = (shrink * inverse, inverse)

    def back(at, cols, grad_probs, factor):
        probs = weight[at, cols].astype(F32) * factor[:, cols]
        grad_logits = (probs * (grad_probs - row_dot[:, cols])).astype(BF16)
        weight[at, cols] = grad_logits
        grad_vals = dot(probs.astype(BF16), grads[cols, :], 1, 0)
        grad_keys = dot(grad_logits, queries[cols, :], 1, 0) * SCALE
        return grad_keys, grad_vals

    def prefix_back(half, core):
        at = chunk_of(half, core)
        if half == 0:
            grad_probs = gradp[at, :]
        else:
            grad_probs = dot(kvs[at, HD : 2 * HD], grads[...], 1, 1)
        return back(at, slice(0, ROWS), grad_probs, factors[half])

    def ship(source, target, index, to):
        copy = pltpu.make_async_remote_copy(
            src_ref=source,
            dst_ref=target,
            send_sem=sum_send_sem.at[index],
            recv_sem=sum_recv_sem.at[index],
            device_id={"roll": device(*to)},
            device_id_type=MESH,
        )
        copy.start()
        return copy

    sums = {}

    def send_core(half):
        grad_keys, grad_vals = prefix_back(half, 1)
        to_core[half, :, 0:HD] = grad_keys.astype(BF16)
        to_core[half, :, HD : 2 * HD] = grad_vals.astype(BF16)
        sums["core", half] = ship(to_core.at[half], from_core.at[half], half, (0, 1, 0))

    def send_row(half):
        grad_keys, grad_vals = prefix_back(half, 0)
        own_sum[half, :, 0:HD] = grad_keys
        own_sum[half, :, HD : 2 * HD] = grad_vals
        sums["core", half].wait_recv()
        for place in (2, 1, 3):
            at = pl.ds(place * BLOCK, BLOCK)
            total = own_sum[half, at, :] + from_core[half, at, :].astype(F32)
            to_row[half, place] = total.astype(BF16)
            sums["row", half, place] = ship(
                to_row.at[half, place],
                from_row.at[half, place],
                CORES + half * ROW + place,
                (0, 0, place),
            )

    def row_total(half):
        at = pl.ds(0, BLOCK)
        total = own_sum[half, at, :] + from_core[half, at, :].astype(F32)
        for place in (1, 3, 2):
            sums["row", half, place].wait_recv()
            total = total + from_row[half, place].astype(F32)
        return total

    send_core(1)
    send_row(1)
    send_core(0)
    to_half[...] = row_total(1).astype(BF16)
    sums["half"] = ship(to_half, from_half, CORES + HALVES * ROW, (1, 0, 0))
    send_row(0)

    grad_keys, grad_vals = back(
        own_rows, own_cols, gradp[own_rows, own_cols], factors[0]
    )
    roll_dkv[0, :, 0:HD] = grad_keys.astype(BF16)
    roll_dkv[0, :, HD : 2 * HD] = grad_vals.astype(BF16)
    out = out_t.T
    for head in range(HEADS):
        columns = slice(head * HD, (head + 1) * HD)
        roll_out[0, :, columns] = out[head * RESP : (head + 1) * RESP]
        at = ROLL_ROWS + head * BLOCK
        pre_out[:, columns] = out[at : at + BLOCK]
    grad_query = dot(keys_t[:, 0:PREFIX], weight[0:PREFIX, :], 1, 0)
    grad_query = widen(
        grad_query, dot(keys_t[:, own_rows], weight[own_rows, own_cols], 1, 0), jnp.add
    )
    grad_query = (grad_query * SCALE).astype(BF16).T
    for head in range(HEADS):
        columns = slice(head * HD, (head + 1) * HD)
        roll_dq[0, :, columns] = grad_query[head * RESP : (head + 1) * RESP]
        at = ROLL_ROWS + head * BLOCK
        pre_dq[:, columns] = grad_query[at : at + BLOCK]

    total = row_total(0)
    sums["half"].wait_recv()
    pre_dkv[...] = (total + from_half[...].astype(F32)).astype(BF16)
    for copy in (*copies.values(), *sums.values()):
        copy.wait_send()


def on_device(pre_q, pre_kv, roll_q, roll_kv, pre_grad, roll_grad, pre_len, roll_len):
    smem = pl.BlockSpec(memory_space=pltpu.SMEM)
    vmem = pl.BlockSpec(memory_space=pltpu.VMEM)
    anywhere = pl.BlockSpec(memory_space=pl.ANY)
    like = lambda array: jax.ShapeDtypeStruct(array.shape, BF16)
    copies = GROUP
    sums = CORES + HALVES * ROW + 1
    return pl.pallas_call(
        kernel,
        out_shape=(
            like(pre_q),
            like(roll_q),
            like(pre_q),
            like(roll_q),
            like(pre_kv),
            like(roll_kv),
        ),
        in_specs=[smem] * 2 + [anywhere] * 6,
        out_specs=[vmem] * 6,
        scratch_shapes=[
            pltpu.VMEM((RESP, HEADS * HD), BF16),
            pltpu.VMEM((RESP, HEADS * HD), BF16),
            pltpu.VMEM((BLOCK, HEADS * HD), BF16),
            pltpu.VMEM((BLOCK, HEADS * HD), BF16),
            pltpu.VMEM((RESP, 2 * HD), BF16),
            pltpu.VMEM((PREFIX, 2 * HD), BF16),
            pltpu.VMEM((ROWS, HD), BF16),
            pltpu.VMEM((ROWS, HD), BF16),
            pltpu.VMEM((PREFIX + RESP, ROWS), F32),
            pltpu.VMEM((PREFIX + RESP, ROWS), BF16),
            pltpu.VMEM((PREFIX + RESP, ROWS), F32),
            pltpu.VMEM((HD, PREFIX + RESP), BF16),
            pltpu.VMEM((HD, PREFIX + RESP), BF16),
            pltpu.VMEM((HALVES, CHUNK, 2 * HD), BF16),
            pltpu.VMEM((HALVES, CHUNK, 2 * HD), BF16),
            pltpu.VMEM((HALVES, CHUNK, 2 * HD), F32),
            pltpu.VMEM((HALVES, ROW, BLOCK, 2 * HD), BF16),
            pltpu.VMEM((HALVES, ROW, BLOCK, 2 * HD), BF16),
            pltpu.VMEM((BLOCK, 2 * HD), BF16),
            pltpu.VMEM((BLOCK, 2 * HD), BF16),
            pltpu.SemaphoreType.DMA((6,)),
            pltpu.SemaphoreType.DMA((copies,)),
            pltpu.SemaphoreType.DMA((copies,)),
            pltpu.SemaphoreType.DMA((sums,)),
            pltpu.SemaphoreType.DMA((sums,)),
        ],
        compiler_params=pltpu.CompilerParams(
            collective_id=0, has_side_effects=True, vmem_limit_bytes=56 << 20
        ),
    )(pre_len, roll_len, pre_q, pre_kv, roll_q, roll_kv, pre_grad, roll_grad)


def solution(mesh):
    in_specs = (
        P(("prompt", "roll"), None),
        P(("prompt", "roll"), None),
        P(("prompt", "roll"), None, None),
        P(("prompt", "roll"), None, None),
        P(("prompt", "roll"), None),
        P(("prompt", "roll"), None, None),
        P("prompt"),
        P(("prompt", "roll")),
    )
    out_specs = (
        P(("prompt", "roll"), None),
        P(("prompt", "roll"), None, None),
        P(("prompt", "roll"), None),
        P(("prompt", "roll"), None, None),
        P(("prompt", "roll"), None),
        P(("prompt", "roll"), None, None),
    )
    return jax.shard_map(
        on_device, mesh=mesh, in_specs=in_specs, out_specs=out_specs, check_vma=False
    )
```

```python
import functools

import jax
import jax.numpy as jnp
from jax import lax
from jax.experimental import pallas as pl
from jax.experimental.pallas import tpu as pltpu
from jax.sharding import PartitionSpec as P

F32 = jnp.float32
BF16 = jnp.bfloat16
MESH = pl.DeviceIdType.MESH
masked_score = -1e30
HALVES, ROW, CORES = 2, 4, 2
BLOCK = 64
RESP = 128
HEADS = 8
HD = 128
GROUP = HALVES * ROW * CORES
CHUNK = ROW * BLOCK
PREFIX = GROUP * BLOCK
ROLL_ROWS = HEADS * RESP
ROWS = HEADS * (RESP + BLOCK)
SCALE = HD**-0.5
LOG2E = 1.4426950408889634


def dot(left, right, left_dim, right_dim):
    return lax.dot_general(
        left, right, (((left_dim,), (right_dim,)), ((), ())), preferred_element_type=F32
    )


def slot(half, core, place):
    return (half * CORES + core) * ROW + place


def block_of(half, core, place):
    return pl.ds(slot(half, core, place) * BLOCK, BLOCK)


def chunk_of(half, core):
    return pl.ds((half * CORES + core) * CHUNK, CHUNK)


def fold8(values, combine):
    return combine(values.reshape(values.shape[0] // 8, 8, values.shape[1]), axis=0)


def kernel(
    pre_len_ref,
    roll_len_ref,
    pre_q,
    pre_kv,
    roll_q,
    roll_kv,
    pre_grad,
    roll_grad,
    pre_out,
    roll_out,
    pre_dq,
    roll_dq,
    pre_dkv,
    roll_dkv,
    rq,
    rg,
    pq,
    pg,
    rkv,
    kvs,
    queries,
    grads,
    score,
    weight,
    gradp,
    keys_t,
    vals_t,
    to_core,
    from_core,
    own_sum,
    to_row,
    from_row,
    to_half,
    from_half,
    load_sem,
    send_sem,
    recv_sem,
    sum_send_sem,
    sum_recv_sem,
):
    me = lax.axis_index("roll")
    my_half, my_place, my_core = me // (ROW * CORES), (me // CORES) % ROW, me % CORES

    def device(half, core, place):
        return (
            ((my_half + half) % HALVES) * (ROW * CORES)
            + ((my_place + place) % ROW) * CORES
            + (my_core + core) % CORES
        )

    partners = [(1, 0, 0), (0, 1, 0), (0, 0, 1), (0, 0, 3), (0, 0, 2)]
    barrier = pltpu.get_barrier_semaphore()
    for partner in partners:
        pl.semaphore_signal(
            barrier, inc=1, device_id={"roll": device(*partner)}, device_id_type=MESH
        )

    loads = []
    for index, (source, target) in enumerate(
        (
            (pre_kv, kvs.at[block_of(0, 0, 0)]),
            (roll_kv.at[0], rkv),
            (roll_q.at[0], rq),
            (pre_q, pq),
            (roll_grad.at[0], rg),
            (pre_grad, pg),
        )
    ):
        loads.append(pltpu.make_async_copy(source, target, load_sem.at[index]))
        loads[-1].start()

    def push(source, half, core, place, to):
        at = slot(half, core, place)
        copy = pltpu.make_async_remote_copy(
            src_ref=source,
            dst_ref=kvs.at[block_of(half, core, place)],
            send_sem=send_sem.at[at],
            recv_sem=recv_sem.at[at],
            device_id={"roll": device(*to)},
            device_id_type=MESH,
        )
        copy.start()
        return copy

    pl.semaphore_wait(barrier, len(partners))
    copies = {}
    copies[1, 0, 0] = push(pre_kv, 1, 0, 0, (1, 0, 0))
    for place in (1, 3, 2):
        copies[0, 0, ROW - place] = push(pre_kv, 0, 0, ROW - place, (0, 0, place))
    copies[0, 1, 0] = push(pre_kv, 0, 1, 0, (0, 1, 0))

    pre_len = pre_len_ref[0]
    roll_len = roll_len_ref[0]
    lane = lax.broadcasted_iota(jnp.int32, (1, ROWS), 1)
    is_roll = lane < ROLL_ROWS
    query_pos = me * BLOCK + lane % BLOCK
    limit = jnp.where(is_roll, pre_len - 1, jnp.minimum(query_pos, pre_len - 1))
    own_limit = jnp.minimum(lane[:, :ROLL_ROWS] % RESP, roll_len - 1)
    rows_left = jnp.where(is_roll, roll_len - lane % RESP, pre_len - query_pos)

    for load in loads:
        load.wait()
    roll_live = lax.broadcasted_iota(jnp.int32, (RESP, HD), 0) < roll_len
    pre_live = lax.broadcasted_iota(jnp.int32, (BLOCK, HD), 0) + me * BLOCK < pre_len
    none = jnp.zeros((), BF16)
    for head in range(HEADS):
        columns = slice(head * HD, (head + 1) * HD)
        at = pl.ds(head * RESP, RESP)
        queries[at, :] = rq[:, columns]
        grads[at, :] = jnp.where(roll_live, rg[:, columns], none)
        at = pl.ds(ROLL_ROWS + head * BLOCK, BLOCK)
        queries[at, :] = pq[:, columns]
        grads[at, :] = jnp.where(pre_live, pg[:, columns], none)

    own_rows = pl.ds(PREFIX, RESP)
    own_cols = slice(0, ROLL_ROWS)

    def transpose_in(half, core):
        at = chunk_of(half, core)
        keys_t[:, at] = kvs[at, 0:HD].T
        vals_t[:, at] = kvs[at, HD : 2 * HD].T

    def scores_of(half, core):
        at = chunk_of(half, core)
        row = lax.broadcasted_iota(jnp.int32, (CHUNK, 1), 0)
        owner = (
            ((my_half + half) % HALVES) * (ROW * CORES)
            + ((my_place + row // BLOCK) % ROW) * CORES
            + (my_core + core) % CORES
        )
        key_pos = owner * BLOCK + row % BLOCK
        logits = dot(kvs[at, 0:HD], queries[...], 1, 1) * (SCALE * LOG2E)
        logits = jnp.where(key_pos <= limit, logits, masked_score)
        score[at, :] = logits
        return fold8(logits, jnp.max)

    def widen(total, own, combine):
        return jnp.concatenate([combine(total[:, own_cols], own), total[:, ROLL_ROWS:]], axis=1)

    def expo_of(half, core, row_max):
        at = chunk_of(half, core)
        expo = jnp.exp2(score[at, :] - row_max)
        rounded = expo.astype(BF16)
        weight[at, :] = rounded
        return fold8(expo, jnp.sum), dot(vals_t[:, at], rounded, 1, 0)

    own_key = lax.broadcasted_iota(jnp.int32, (RESP, 1), 0)
    own_logits = dot(rkv[:, 0:HD], queries[own_cols, :], 1, 1) * (SCALE * LOG2E)
    own_logits = jnp.where(own_key <= own_limit, own_logits, masked_score)
    score[own_rows, own_cols] = own_logits
    own_max = fold8(own_logits, jnp.max)
    keys_t[:, own_rows] = rkv[:, 0:HD].T
    vals_t[:, own_rows] = rkv[:, HD : 2 * HD].T
    gradp[own_rows, own_cols] = dot(rkv[:, HD : 2 * HD], grads[own_cols, :], 1, 1)
    grad_t = grads[...].T.astype(F32)

    for place in (1, 3, 2):
        copies[0, 0, place].wait_recv()
        copies[0, 1, place] = push(
            kvs.at[block_of(0, 0, place)], 0, 1, place, (0, 1, 0)
        )
    transpose_in(0, 0)
    near_max = scores_of(0, 0)
    copies[1, 0, 0].wait_recv()
    for place in (1, 3, 2):
        copies[1, 0, ROW - place] = push(
            kvs.at[block_of(1, 0, 0)], 1, 0, ROW - place, (0, 0, place)
        )
    copies[1, 1, 0] = push(kvs.at[block_of(1, 0, 0)], 1, 1, 0, (0, 1, 0))
    for place in range(ROW):
        copies[0, 1, place].wait_recv()
    transpose_in(0, 1)
    near_max = jnp.maximum(near_max, scores_of(0, 1))
    near_max = widen(near_max, own_max, jnp.maximum)
    near_max = jnp.max(near_max, axis=0, keepdims=True)
    for place in (1, 3, 2):
        copies[1, 0, place].wait_recv()
        copies[1, 1, place] = push(
            kvs.at[block_of(1, 0, place)], 1, 1, place, (0, 1, 0)
        )
    near_sum, near_out = expo_of(0, 0, near_max)
    more_sum, more_out = expo_of(0, 1, near_max)
    near_sum, near_out = near_sum + more_sum, near_out + more_out
    expo = jnp.exp2(score[own_rows, own_cols] - near_max[:, own_cols])
    rounded = expo.astype(BF16)
    weight[own_rows, own_cols] = rounded
    near_sum = widen(near_sum, fold8(expo, jnp.sum), jnp.add)
    near_out = widen(near_out, dot(vals_t[:, own_rows], rounded, 1, 0), jnp.add)
    near_sum = jnp.sum(near_sum, axis=0, keepdims=True)
    for core in range(CORES):
        at = chunk_of(0, core)
        gradp[at, :] = dot(kvs[at, HD : 2 * HD], grads[...], 1, 1)

    transpose_in(1, 0)
    far_max = scores_of(1, 0)
    for place in range(ROW):
        copies[1, 1, place].wait_recv()
    transpose_in(1, 1)
    far_max = jnp.maximum(far_max, scores_of(1, 1))
    far_max = jnp.max(far_max, axis=0, keepdims=True)
    row_max = jnp.maximum(near_max, far_max)
    shrink = jnp.exp2(near_max - row_max)
    far_sum, far_out = expo_of(1, 0, row_max)
    more_sum, more_out = expo_of(1, 1, row_max)
    far_sum = jnp.sum(far_sum + more_sum, axis=0, keepdims=True)
    row_sum = near_sum * shrink + far_sum
    inverse = 1.0 / row_sum
    out_t = near_out * shrink + (far_out + more_out)
    out_t = (out_t * jnp.where(rows_left > 0, inverse, 0.0)).astype(BF16)
    row_dot = jnp.sum(grad_t * out_t.astype(F32), axis=0, keepdims=True)
    factors = (shrink * inverse, inverse)

    def back(at, cols, grad_probs, factor):
        probs = weight[at, cols].astype(F32) * factor[:, cols]
        grad_logits = (probs * (grad_probs - row_dot[:, cols])).astype(BF16)
        weight[at, cols] = grad_logits
        grad_vals = dot(probs.astype(BF16), grads[cols, :], 1, 0)
        grad_keys = dot(grad_logits, queries[cols, :], 1, 0) * SCALE
        return grad_keys, grad_vals

    def prefix_back(half, core):
        at = chunk_of(half, core)
        if half == 0:
            grad_probs = gradp[at, :]
        else:
            grad_probs = dot(kvs[at, HD : 2 * HD], grads[...], 1, 1)
        return back(at, slice(0, ROWS), grad_probs, factors[half])

    def ship(source, target, index, to):
        copy = pltpu.make_async_remote_copy(
            src_ref=source,
            dst_ref=target,
            send_sem=sum_send_sem.at[index],
            recv_sem=sum_recv_sem.at[index],
            device_id={"roll": device(*to)},
            device_id_type=MESH,
        )
        copy.start()
        return copy

    sums = {}

    def send_core(half):
        grad_keys, grad_vals = prefix_back(half, 1)
        to_core[half, :, 0:HD] = grad_keys.astype(BF16)
        to_core[half, :, HD : 2 * HD] = grad_vals.astype(BF16)
        sums["core", half] = ship(to_core.at[half], from_core.at[half], half, (0, 1, 0))

    def send_row(half):
        grad_keys, grad_vals = prefix_back(half, 0)
        own_sum[half, :, 0:HD] = grad_keys
        own_sum[half, :, HD : 2 * HD] = grad_vals
        sums["core", half].wait_recv()
        for place in (2, 1, 3):
            at = pl.ds(place * BLOCK, BLOCK)
            total = own_sum[half, at, :] + from_core[half, at, :].astype(F32)
            to_row[half, place] = total.astype(BF16)
            sums["row", half, place] = ship(
                to_row.at[half, place],
                from_row.at[half, place],
                CORES + half * ROW + place,
                (0, 0, place),
            )

    def row_total(half):
        at = pl.ds(0, BLOCK)
        total = own_sum[half, at, :] + from_core[half, at, :].astype(F32)
        for place in (1, 3, 2):
            sums["row", half, place].wait_recv()
            total = total + from_row[half, place].astype(F32)
        return total

    send_core(1)
    send_row(1)
    send_core(0)
    to_half[...] = row_total(1).astype(BF16)
    sums["half"] = ship(to_half, from_half, CORES + HALVES * ROW, (1, 0, 0))
    send_row(0)

    grad_keys, grad_vals = back(
        own_rows, own_cols, gradp[own_rows, own_cols], factors[0]
    )
    roll_dkv[0, :, 0:HD] = grad_keys.astype(BF16)
    roll_dkv[0, :, HD : 2 * HD] = grad_vals.astype(BF16)
    out = out_t.T
    for head in range(HEADS):
        columns = slice(head * HD, (head + 1) * HD)
        roll_out[0, :, columns] = out[head * RESP : (head + 1) * RESP]
        at = ROLL_ROWS + head * BLOCK
        pre_out[:, columns] = out[at : at + BLOCK]
    grad_query = dot(keys_t[:, 0:PREFIX], weight[0:PREFIX, :], 1, 0)
    grad_query = widen(
        grad_query, dot(keys_t[:, own_rows], weight[own_rows, own_cols], 1, 0), jnp.add
    )
    grad_query = (grad_query * SCALE).astype(BF16).T
    for head in range(HEADS):
        columns = slice(head * HD, (head + 1) * HD)
        roll_dq[0, :, columns] = grad_query[head * RESP : (head + 1) * RESP]
        at = ROLL_ROWS + head * BLOCK
        pre_dq[:, columns] = grad_query[at : at + BLOCK]

    total = row_total(0)
    sums["half"].wait_recv()
    pre_dkv[...] = (total + from_half[...].astype(F32)).astype(BF16)
    for copy in (*copies.values(), *sums.values()):
        copy.wait_send()


def drain(*refs):
    count = (len(refs) - 1) // 2
    sem = refs[-1]
    copies = [
        pltpu.make_async_copy(refs[index], refs[count + index], sem.at[index])
        for index in range(count)
    ]
    for copy in copies:
        copy.start()
    for copy in copies:
        copy.wait()


def on_device(pre_q, pre_kv, roll_q, roll_kv, pre_grad, roll_grad, pre_len, roll_len):
    smem = pl.BlockSpec(memory_space=pltpu.SMEM)
    vmem = pl.BlockSpec(memory_space=pltpu.VMEM)
    anywhere = pl.BlockSpec(memory_space=pl.ANY)
    like = lambda array: pltpu.VMEM(array.shape, BF16)
    final = lambda array: jax.ShapeDtypeStruct(array.shape, BF16)
    copies = GROUP
    sums = CORES + HALVES * ROW + 1
    results = pl.pallas_call(
        kernel,
        out_shape=(
            like(pre_q),
            like(roll_q),
            like(pre_q),
            like(roll_q),
            like(pre_kv),
            like(roll_kv),
        ),
        in_specs=[smem] * 2 + [anywhere] * 6,
        out_specs=[vmem] * 6,
        scratch_shapes=[
            pltpu.VMEM((RESP, HEADS * HD), BF16),
            pltpu.VMEM((RESP, HEADS * HD), BF16),
            pltpu.VMEM((BLOCK, HEADS * HD), BF16),
            pltpu.VMEM((BLOCK, HEADS * HD), BF16),
            pltpu.VMEM((RESP, 2 * HD), BF16),
            pltpu.VMEM((PREFIX, 2 * HD), BF16),
            pltpu.VMEM((ROWS, HD), BF16),
            pltpu.VMEM((ROWS, HD), BF16),
            pltpu.VMEM((PREFIX + RESP, ROWS), F32),
            pltpu.VMEM((PREFIX + RESP, ROWS), BF16),
            pltpu.VMEM((PREFIX + RESP, ROWS), F32),
            pltpu.VMEM((HD, PREFIX + RESP), BF16),
            pltpu.VMEM((HD, PREFIX + RESP), BF16),
            pltpu.VMEM((HALVES, CHUNK, 2 * HD), BF16),
            pltpu.VMEM((HALVES, CHUNK, 2 * HD), BF16),
            pltpu.VMEM((HALVES, CHUNK, 2 * HD), F32),
            pltpu.VMEM((HALVES, ROW, BLOCK, 2 * HD), BF16),
            pltpu.VMEM((HALVES, ROW, BLOCK, 2 * HD), BF16),
            pltpu.VMEM((BLOCK, 2 * HD), BF16),
            pltpu.VMEM((BLOCK, 2 * HD), BF16),
            pltpu.SemaphoreType.DMA((6,)),
            pltpu.SemaphoreType.DMA((copies,)),
            pltpu.SemaphoreType.DMA((copies,)),
            pltpu.SemaphoreType.DMA((sums,)),
            pltpu.SemaphoreType.DMA((sums,)),
        ],
        compiler_params=pltpu.CompilerParams(
            collective_id=0, has_side_effects=True, vmem_limit_bytes=56 << 20
        ),
    )(pre_len, roll_len, pre_q, pre_kv, roll_q, roll_kv, pre_grad, roll_grad)
    return pl.pallas_call(
        drain,
        out_shape=tuple(final(array) for array in (pre_q, roll_q, pre_q, roll_q, pre_kv, roll_kv)),
        in_specs=[vmem] * 6,
        out_specs=[anywhere] * 6,
        scratch_shapes=[pltpu.SemaphoreType.DMA((6,))],
    )(*(pltpu.with_memory_space_constraint(result, pltpu.VMEM) for result in results))


def solution(mesh):
    in_specs = (
        P(("prompt", "roll"), None),
        P(("prompt", "roll"), None),
        P(("prompt", "roll"), None, None),
        P(("prompt", "roll"), None, None),
        P(("prompt", "roll"), None),
        P(("prompt", "roll"), None, None),
        P("prompt"),
        P(("prompt", "roll")),
    )
    out_specs = (
        P(("prompt", "roll"), None),
        P(("prompt", "roll"), None, None),
        P(("prompt", "roll"), None),
        P(("prompt", "roll"), None, None),
        P(("prompt", "roll"), None),
        P(("prompt", "roll"), None, None),
    )
    return jax.shard_map(
        on_device, mesh=mesh, in_specs=in_specs, out_specs=out_specs, check_vma=False
    )
```

```python
import functools

import jax
import jax.numpy as jnp
from jax import lax
from jax.experimental import pallas as pl
from jax.experimental.pallas import tpu as pltpu
from jax.sharding import PartitionSpec as P

F32 = jnp.float32
BF16 = jnp.bfloat16
MESH = pl.DeviceIdType.MESH
masked_score = -1e30
HALVES, ROW, CORES = 2, 4, 2
BLOCK = 64
RESP = 128
HEADS = 8
HD = 128
GROUP = HALVES * ROW * CORES
PREFIX = GROUP * BLOCK
ROLL_ROWS = HEADS * RESP
ROWS = HEADS * (RESP + BLOCK)
SCALE = HD**-0.5
LOG2E = 1.4426950408889634


def dot(left, right, left_dim, right_dim):
    return lax.dot_general(
        left, right, (((left_dim,), (right_dim,)), ((), ())), preferred_element_type=F32
    )


POS = (0, 1, 3, 2)


def slot(half, place, core):
    return (half * ROW + POS[place]) * CORES + core


def rows_of(half, place, core):
    return pl.ds(slot(half, place, core) * BLOCK, BLOCK)


def fold8(values, combine):
    return combine(values.reshape(values.shape[0] // 8, 8, values.shape[1]), axis=0)


def kernel(
    pre_len_ref,
    roll_len_ref,
    pre_q,
    pre_kv,
    roll_q,
    roll_kv,
    pre_grad,
    roll_grad,
    pre_out,
    roll_out,
    pre_dq,
    roll_dq,
    pre_dkv,
    roll_dkv,
    rq,
    rg,
    pq,
    pg,
    rkv,
    kvs,
    queries,
    grads,
    score,
    weight,
    gradp,
    keys_t,
    vals_t,
    to_core,
    from_core,
    own_sum,
    to_owner,
    from_owner,
    load_sem,
    send_sem,
    recv_sem,
    sum_send_sem,
    sum_recv_sem,
):
    me = lax.axis_index("roll")
    my_half, my_place, my_core = me // (ROW * CORES), (me // CORES) % ROW, me % CORES

    def device(half, place, core):
        return (
            ((my_half + half) % HALVES) * (ROW * CORES)
            + ((my_place + place) % ROW) * CORES
            + (my_core + core) % CORES
        )

    partners = [(1, 0, 0), (0, 0, 1), (0, 1, 0), (0, 3, 0), (0, 2, 0)]
    barrier = pltpu.get_barrier_semaphore()
    for partner in partners:
        pl.semaphore_signal(
            barrier, inc=1, device_id={"roll": device(*partner)}, device_id_type=MESH
        )

    loads = []
    for index, (source, target) in enumerate(
        (
            (pre_kv, kvs.at[rows_of(0, 0, 0)]),
            (roll_kv.at[0], rkv),
            (roll_q.at[0], rq),
            (pre_q, pq),
            (roll_grad.at[0], rg),
            (pre_grad, pg),
        )
    ):
        loads.append(pltpu.make_async_copy(source, target, load_sem.at[index]))
        loads[-1].start()

    copies = {}

    def push(source, block, to):
        at = slot(*block)
        copies[block] = pltpu.make_async_remote_copy(
            src_ref=source,
            dst_ref=kvs.at[rows_of(*block)],
            send_sem=send_sem.at[at],
            recv_sem=recv_sem.at[at],
            device_id={"roll": device(*to)},
            device_id_type=MESH,
        )
        copies[block].start()

    def relay(half, place):
        push(kvs.at[rows_of(half, place, 0)], (half, place, 1), (0, 0, 1))

    loads[0].wait()
    pl.semaphore_wait(barrier, len(partners))
    held = kvs.at[rows_of(0, 0, 0)]
    push(held, (1, 0, 0), (1, 0, 0))
    for place in (2, 1, 3):
        push(held, (0, ROW - place, 0), (0, place, 0))
    push(held, (0, 0, 1), (0, 0, 1))

    pre_len = pre_len_ref[0]
    roll_len = roll_len_ref[0]
    lane = lax.broadcasted_iota(jnp.int32, (1, ROWS), 1)
    is_roll = lane < ROLL_ROWS
    query_pos = me * BLOCK + lane % BLOCK
    limit = jnp.where(is_roll, pre_len - 1, jnp.minimum(query_pos, pre_len - 1))
    own_limit = jnp.minimum(lane[:, :ROLL_ROWS] % RESP, roll_len - 1)
    rows_left = jnp.where(is_roll, roll_len - lane % RESP, pre_len - query_pos)

    for load in loads[1:]:
        load.wait()
    for head in range(HEADS):
        columns = slice(head * HD, (head + 1) * HD)
        at = pl.ds(head * RESP, RESP)
        queries[at, :] = rq[:, columns]
        grads[at, :] = rg[:, columns]
        at = pl.ds(ROLL_ROWS + head * BLOCK, BLOCK)
        queries[at, :] = pq[:, columns]
        grads[at, :] = pg[:, columns]

    own_rows = pl.ds(PREFIX, RESP)
    all_cols = slice(0, ROWS)
    own_cols = slice(0, ROLL_ROWS)

    def take(first, count):
        at = pl.ds(first, count)
        keys_t[:, at] = kvs[at, 0:HD].T
        vals_t[:, at] = kvs[at, HD : 2 * HD].T
        row = lax.broadcasted_iota(jnp.int32, (count, 1), 0) + first
        half = row // (PREFIX // HALVES)
        order = row // (CORES * BLOCK) % ROW
        place = order ^ (order >> 1)
        core = row // BLOCK % CORES
        owner = (
            ((my_half + half) % HALVES) * (ROW * CORES)
            + ((my_place + place) % ROW) * CORES
            + (my_core + core) % CORES
        )
        key_pos = owner * BLOCK + row % BLOCK
        logits = dot(kvs[at, 0:HD], queries[...], 1, 1) * (SCALE * LOG2E)
        logits = jnp.where(key_pos <= limit, logits, masked_score)
        score[at, :] = logits
        return fold8(logits, jnp.max)

    def widen(total, own, combine):
        return jnp.concatenate([combine(total[:, own_cols], own), total[:, ROLL_ROWS:]], axis=1)

    def weigh(at, cols, row_max):
        expo = jnp.exp2(score[at, cols] - row_max)
        rounded = expo.astype(BF16)
        weight[at, cols] = rounded
        return fold8(expo, jnp.sum), dot(vals_t[:, at], rounded, 1, 0)

    def grad_probs_of(at):
        return dot(kvs[at, HD : 2 * HD], grads[...], 1, 1)

    own_key = lax.broadcasted_iota(jnp.int32, (RESP, 1), 0)
    own_logits = dot(rkv[:, 0:HD], queries[own_cols, :], 1, 1) * (SCALE * LOG2E)
    own_logits = jnp.where(own_key <= own_limit, own_logits, masked_score)
    score[own_rows, own_cols] = own_logits
    own_max = fold8(own_logits, jnp.max)
    keys_t[:, own_rows] = rkv[:, 0:HD].T
    vals_t[:, own_rows] = rkv[:, HD : 2 * HD].T
    gradp[own_rows, own_cols] = dot(rkv[:, HD : 2 * HD], grads[own_cols, :], 1, 1)
    grad_t = grads[...].T.astype(F32)

    pair = CORES * BLOCK
    for place in (1, 3, 2):
        copies[0, place, 0].wait_recv()
        relay(0, place)
    copies[0, 0, 1].wait_recv()
    copies[0, 1, 1].wait_recv()
    near_max = take(0, 2 * pair)
    copies[1, 0, 0].wait_recv()
    for place in (2, 1, 3):
        push(kvs.at[rows_of(1, 0, 0)], (1, ROW - place, 0), (0, place, 0))
    relay(1, 0)
    copies[0, 3, 1].wait_recv()
    copies[0, 2, 1].wait_recv()
    near_max = jnp.maximum(near_max, take(2 * pair, 2 * pair))
    near_max = widen(near_max, own_max, jnp.maximum)
    row_max = jnp.max(near_max, axis=0, keepdims=True)
    near = pl.ds(0, ROW * pair)
    row_sum, out_t = weigh(near, all_cols, row_max)
    own_sum_8, own_out = weigh(own_rows, own_cols, row_max[:, own_cols])
    row_sum = jnp.sum(widen(row_sum, own_sum_8, jnp.add), axis=0, keepdims=True)
    out_t = widen(out_t, own_out, jnp.add)
    phase_max = [row_max]
    gradp[near, :] = grad_probs_of(near)

    def fold_in(first, count, state):
        row_max, row_sum, out_t = state
        new_max = jnp.max(take(first, count), axis=0, keepdims=True)
        new_max = jnp.maximum(row_max, new_max)
        shrink = jnp.exp2(row_max - new_max)
        more_sum, more_out = weigh(pl.ds(first, count), all_cols, new_max)
        phase_max.append(new_max)
        row_sum = row_sum * shrink + jnp.sum(more_sum, axis=0, keepdims=True)
        return new_max, row_sum, out_t * shrink + more_out

    far = ROW * pair
    copies[1, 0, 1].wait_recv()
    state = fold_in(far, pair, (row_max, row_sum, out_t))
    gradp[pl.ds(far, pair), :] = grad_probs_of(pl.ds(far, pair))
    for place in (1, 3, 2):
        copies[1, place, 0].wait_recv()
        relay(1, place)
    copies[1, 1, 1].wait_recv()
    copies[1, 3, 1].wait_recv()
    state = fold_in(far + pair, 2 * pair, state)
    copies[1, 2, 1].wait_recv()
    row_max, row_sum, out_t = fold_in(far + 3 * pair, pair, state)

    inverse = jnp.where(rows_left > 0, 1.0 / row_sum, 0.0)
    out_t = (out_t * inverse).astype(BF16)
    row_dot = jnp.sum(grad_t * out_t.astype(F32), axis=0, keepdims=True)
    factors = [jnp.exp2(past - row_max) * inverse for past in phase_max]

    def back(at, cols, grad_probs, factor):
        probs = weight[at, cols].astype(F32) * factor[:, cols]
        grad_logits = (probs * (grad_probs - row_dot[:, cols])).astype(BF16)
        weight[at, cols] = grad_logits
        grad_vals = dot(probs.astype(BF16), grads[cols, :], 1, 0)
        grad_keys = dot(grad_logits, queries[cols, :], 1, 0) * SCALE
        return grad_keys, grad_vals

    def ship(source, target, index, to):
        copy = pltpu.make_async_remote_copy(
            src_ref=source,
            dst_ref=target,
            send_sem=sum_send_sem.at[index],
            recv_sem=sum_recv_sem.at[index],
            device_id={"roll": device(*to)},
            device_id_type=MESH,
        )
        copy.start()
        return copy

    sums = {}

    def prefix_back(first, count, grad_probs, factor):
        grad_keys, grad_vals = back(pl.ds(first, count), all_cols, grad_probs, factor)
        for pairs in range(count // pair):
            at = first // pair + pairs
            rows = slice(pairs * pair, pairs * pair + BLOCK)
            own_sum[at, :, 0:HD] = grad_keys[rows]
            own_sum[at, :, HD : 2 * HD] = grad_vals[rows]
            rows = slice(pairs * pair + BLOCK, (pairs + 1) * pair)
            to_core[at, :, 0:HD] = grad_keys[rows].astype(BF16)
            to_core[at, :, HD : 2 * HD] = grad_vals[rows].astype(BF16)
            sums["core", at] = ship(to_core.at[at], from_core.at[at], at, (0, 0, 1))

    def chip_total(at):
        sums["core", at].wait_recv()
        return own_sum[at] + from_core[at].astype(F32)

    def send_on(half, place, to):
        at = half * ROW + POS[place]
        to_owner[at] = chip_total(at).astype(BF16)
        lands = half * ROW + POS[(ROW - place) % ROW]
        sums["owner", lands] = ship(
            to_owner.at[at], from_owner.at[lands], HALVES * ROW + lands, to
        )

    last = pl.ds(far + 3 * pair, pair)
    middle = pl.ds(far + pair, 2 * pair)
    prefix_back(far + pair, 2 * pair, grad_probs_of(middle), factors[2])
    prefix_back(far + 3 * pair, pair, grad_probs_of(last), factors[3])
    send_on(1, 1, (0, 1, 0))
    send_on(1, 3, (0, 3, 0))
    prefix_back(far, pair, gradp[pl.ds(far, pair), :], factors[1])
    send_on(1, 2, (1, 2, 0))
    prefix_back(2 * pair, 2 * pair, gradp[pl.ds(2 * pair, 2 * pair), :], factors[0])
    prefix_back(0, 2 * pair, gradp[pl.ds(0, 2 * pair), :], factors[0])
    send_on(0, 2, (0, 2, 0))
    send_on(0, 3, (0, 3, 0))
    send_on(0, 1, (0, 1, 0))

    total = chip_total(ROW)
    for place in (1, 3):
        at = ROW + POS[place]
        sums["owner", at].wait_recv()
        total = total + from_owner[at].astype(F32)
    to_owner[ROW] = total.astype(BF16)
    sums["owner", ROW] = ship(
        to_owner.at[ROW], from_owner.at[ROW], HALVES * ROW + ROW, (1, 0, 0)
    )

    grad_keys, grad_vals = back(
        own_rows, own_cols, gradp[own_rows, own_cols], factors[0]
    )
    roll_dkv[0, :, 0:HD] = grad_keys.astype(BF16)
    roll_dkv[0, :, HD : 2 * HD] = grad_vals.astype(BF16)
    out = out_t.T
    for head in range(HEADS):
        columns = slice(head * HD, (head + 1) * HD)
        roll_out[0, :, columns] = out[head * RESP : (head + 1) * RESP]
        at = ROLL_ROWS + head * BLOCK
        pre_out[:, columns] = out[at : at + BLOCK]
    grad_query = dot(keys_t[:, 0:PREFIX], weight[0:PREFIX, :], 1, 0)
    grad_query = widen(
        grad_query, dot(keys_t[:, own_rows], weight[own_rows, own_cols], 1, 0), jnp.add
    )
    grad_query = (grad_query * SCALE).astype(BF16).T
    for head in range(HEADS):
        columns = slice(head * HD, (head + 1) * HD)
        roll_dq[0, :, columns] = grad_query[head * RESP : (head + 1) * RESP]
        at = ROLL_ROWS + head * BLOCK
        pre_dq[:, columns] = grad_query[at : at + BLOCK]

    total = chip_total(0)
    for at in (1, 2, 3, ROW + POS[2], ROW):
        sums["owner", at].wait_recv()
        total = total + from_owner[at].astype(F32)
    pre_dkv[...] = total.astype(BF16)
    for copy in (*copies.values(), *sums.values()):
        copy.wait_send()


def drain(*refs):
    count = (len(refs) - 1) // 2
    sem = refs[-1]
    copies = [
        pltpu.make_async_copy(refs[index], refs[count + index], sem.at[index])
        for index in range(count)
    ]
    for copy in copies:
        copy.start()
    for copy in copies:
        copy.wait()


def on_device(pre_q, pre_kv, roll_q, roll_kv, pre_grad, roll_grad, pre_len, roll_len):
    smem = pl.BlockSpec(memory_space=pltpu.SMEM)
    vmem = pl.BlockSpec(memory_space=pltpu.VMEM)
    anywhere = pl.BlockSpec(memory_space=pl.ANY)
    like = lambda array: pltpu.VMEM(array.shape, BF16)
    final = lambda array: jax.ShapeDtypeStruct(array.shape, BF16)
    copies = GROUP
    sums = 2 * HALVES * ROW
    results = pl.pallas_call(
        kernel,
        out_shape=(
            like(pre_q),
            like(roll_q),
            like(pre_q),
            like(roll_q),
            like(pre_kv),
            like(roll_kv),
        ),
        in_specs=[smem] * 2 + [anywhere] * 6,
        out_specs=[vmem] * 6,
        scratch_shapes=[
            pltpu.VMEM((RESP, HEADS * HD), BF16),
            pltpu.VMEM((RESP, HEADS * HD), BF16),
            pltpu.VMEM((BLOCK, HEADS * HD), BF16),
            pltpu.VMEM((BLOCK, HEADS * HD), BF16),
            pltpu.VMEM((RESP, 2 * HD), BF16),
            pltpu.VMEM((PREFIX, 2 * HD), BF16),
            pltpu.VMEM((ROWS, HD), BF16),
            pltpu.VMEM((ROWS, HD), BF16),
            pltpu.VMEM((PREFIX + RESP, ROWS), F32),
            pltpu.VMEM((PREFIX + RESP, ROWS), BF16),
            pltpu.VMEM((PREFIX + RESP, ROWS), F32),
            pltpu.VMEM((HD, PREFIX + RESP), BF16),
            pltpu.VMEM((HD, PREFIX + RESP), BF16),
            pltpu.VMEM((HALVES * ROW, BLOCK, 2 * HD), BF16),
            pltpu.VMEM((HALVES * ROW, BLOCK, 2 * HD), BF16),
            pltpu.VMEM((HALVES * ROW, BLOCK, 2 * HD), F32),
            pltpu.VMEM((HALVES * ROW, BLOCK, 2 * HD), BF16),
            pltpu.VMEM((HALVES * ROW, BLOCK, 2 * HD), BF16),
            pltpu.SemaphoreType.DMA((6,)),
            pltpu.SemaphoreType.DMA((copies,)),
            pltpu.SemaphoreType.DMA((copies,)),
            pltpu.SemaphoreType.DMA((sums,)),
            pltpu.SemaphoreType.DMA((sums,)),
        ],
        compiler_params=pltpu.CompilerParams(
            collective_id=0, has_side_effects=True, vmem_limit_bytes=56 << 20
        ),
    )(pre_len, roll_len, pre_q, pre_kv, roll_q, roll_kv, pre_grad, roll_grad)
    return pl.pallas_call(
        drain,
        out_shape=tuple(final(array) for array in (pre_q, roll_q, pre_q, roll_q, pre_kv, roll_kv)),
        in_specs=[vmem] * 6,
        out_specs=[anywhere] * 6,
        scratch_shapes=[pltpu.SemaphoreType.DMA((6,))],
    )(*(pltpu.with_memory_space_constraint(result, pltpu.VMEM) for result in results))


def solution(mesh):
    in_specs = (
        P(("prompt", "roll"), None),
        P(("prompt", "roll"), None),
        P(("prompt", "roll"), None, None),
        P(("prompt", "roll"), None, None),
        P(("prompt", "roll"), None),
        P(("prompt", "roll"), None, None),
        P("prompt"),
        P(("prompt", "roll")),
    )
    out_specs = (
        P(("prompt", "roll"), None),
        P(("prompt", "roll"), None, None),
        P(("prompt", "roll"), None),
        P(("prompt", "roll"), None, None),
        P(("prompt", "roll"), None),
        P(("prompt", "roll"), None, None),
    )
    return jax.shard_map(
        on_device, mesh=mesh, in_specs=in_specs, out_specs=out_specs, check_vma=False
    )
```

```python
import functools

import jax
import jax.numpy as jnp
from jax import lax
from jax.experimental import pallas as pl
from jax.experimental.pallas import tpu as pltpu
from jax.sharding import PartitionSpec as P

F32 = jnp.float32
BF16 = jnp.bfloat16
MESH = pl.DeviceIdType.MESH
masked_score = -1e30
HALVES, ROW, CORES = 2, 4, 2
BLOCK = 64
RESP = 128
HEADS = 8
HD = 128
GROUP = HALVES * ROW * CORES
PREFIX = GROUP * BLOCK
ROLL_ROWS = HEADS * RESP
ROWS = HEADS * (RESP + BLOCK)
SCALE = HD**-0.5
LOG2E = 1.4426950408889634


def dot(left, right, left_dim, right_dim):
    return lax.dot_general(
        left, right, (((left_dim,), (right_dim,)), ((), ())), preferred_element_type=F32
    )


POS = (0, 1, 3, 2)
LAYOUT = ((0, 0), (0, 1), (1, 0), (3, 0), (1, 1), (3, 1), (2, 0), (2, 1))


def slot(half, place, core):
    return half * len(LAYOUT) + LAYOUT.index((place, core))


def blocks_in(first, count):
    slots = range(first // BLOCK, (first + count) // BLOCK)
    return [(at // len(LAYOUT), *LAYOUT[at % len(LAYOUT)]) for at in slots]


def rows_of(half, place, core):
    return pl.ds(slot(half, place, core) * BLOCK, BLOCK)


def fold8(values, combine):
    return combine(values.reshape(values.shape[0] // 8, 8, values.shape[1]), axis=0)


def kernel(
    pre_len_ref,
    roll_len_ref,
    pre_q,
    pre_kv,
    roll_q,
    roll_kv,
    pre_grad,
    roll_grad,
    pre_out,
    roll_out,
    pre_dq,
    roll_dq,
    pre_dkv,
    roll_dkv,
    rq,
    rg,
    pq,
    pg,
    rkv,
    kvs,
    queries,
    grads,
    score,
    weight,
    gradp,
    keys_t,
    vals_t,
    to_core,
    from_core,
    own_sum,
    to_owner,
    from_owner,
    from_row,
    to_opposite,
    load_sem,
    send_sem,
    recv_sem,
    sum_send_sem,
    sum_recv_sem,
):
    me = lax.axis_index("roll")
    my_half, my_place, my_core = me // (ROW * CORES), (me // CORES) % ROW, me % CORES

    def device(half, place, core):
        return (
            ((my_half + half) % HALVES) * (ROW * CORES)
            + ((my_place + place) % ROW) * CORES
            + (my_core + core) % CORES
        )

    speaker = 1 - my_core
    partners = [(1, 0, speaker), (0, 0, 1), (0, 1, 0), (0, 3, 0), (0, 2, 0)]
    barrier = pltpu.get_barrier_semaphore()

    def announce(partner):
        pl.semaphore_signal(
            barrier, inc=1, device_id={"roll": device(*partner)}, device_id_type=MESH
        )

    for partner in partners:
        announce(partner)

    @pl.when(my_core == 1)
    def _():
        announce((1, 0, 1))

    loads = []
    for index, (source, target) in enumerate(
        (
            (pre_kv, kvs.at[rows_of(0, 0, 0)]),
            (roll_kv.at[0], rkv),
            (roll_q.at[0], rq),
            (pre_q, pq),
            (roll_grad.at[0], rg),
            (pre_grad, pg),
        )
    ):
        loads.append(pltpu.make_async_copy(source, target, load_sem.at[index]))
        loads[-1].start()

    def block_copy(source, at, index, to):
        return pltpu.make_async_remote_copy(
            src_ref=source,
            dst_ref=kvs.at[pl.ds(at * BLOCK, BLOCK)],
            send_sem=send_sem.at[index],
            recv_sem=recv_sem.at[at],
            device_id={"roll": device(*to)},
            device_id_type=MESH,
        )

    def push(source, at, index, to):
        copy = block_copy(source, at, index, to)
        copy.start()
        return copy

    def arrived(*block):
        at = slot(*block)
        block_copy(kvs.at[rows_of(*block)], at, 0, (0, 0, 1)).wait_recv()

    def relay_near(place):
        at = slot(0, place, 1)
        copies.append(push(kvs.at[rows_of(0, place, 0)], at, at, (0, 0, 1)))

    def to_sibling(place, core, start=True):
        at = slot(1, place, 1 - core)
        copy = block_copy(kvs.at[rows_of(1, place, core)], at, GROUP + at, (0, 0, 1))
        copy.start() if start else copy.wait_send()

    def along_row(place, core, start=True):
        at = slot(1, ROW - place, core)
        copy = block_copy(kvs.at[rows_of(1, 0, core)], at, GROUP + place * CORES + core, (0, place, 0))
        copy.start() if start else copy.wait_send()

    copies = []
    loads[0].wait()
    pl.semaphore_wait(barrier, len(partners) + my_core)
    held = kvs.at[rows_of(0, 0, 0)]
    copies.append(push(held, slot(1, 0, 0) + speaker, 0, (1, 0, speaker)))
    for place in (2, 1, 3):
        at = slot(0, ROW - place, 0)
        copies.append(push(held, at, at, (0, place, 0)))
    at = slot(0, 0, 1)
    copies.append(push(held, at, at, (0, 0, 1)))

    pre_len = pre_len_ref[0]
    roll_len = roll_len_ref[0]
    lane = lax.broadcasted_iota(jnp.int32, (1, ROWS), 1)
    is_roll = lane < ROLL_ROWS
    query_pos = me * BLOCK + lane % BLOCK
    limit = jnp.where(is_roll, pre_len - 1, jnp.minimum(query_pos, pre_len - 1))
    own_limit = jnp.minimum(lane[:, :ROLL_ROWS] % RESP, roll_len - 1)
    rows_left = jnp.where(is_roll, roll_len - lane % RESP, pre_len - query_pos)

    for load in loads[1:]:
        load.wait()
    for head in range(HEADS):
        columns = slice(head * HD, (head + 1) * HD)
        at = pl.ds(head * RESP, RESP)
        queries[at, :] = rq[:, columns]
        grads[at, :] = rg[:, columns]
        at = pl.ds(ROLL_ROWS + head * BLOCK, BLOCK)
        queries[at, :] = pq[:, columns]
        grads[at, :] = pg[:, columns]

    own_rows = pl.ds(PREFIX, RESP)
    all_cols = slice(0, ROWS)
    own_cols = slice(0, ROLL_ROWS)

    def take(first, count):
        at = pl.ds(first, count)
        keys_t[:, at] = kvs[at, 0:HD].T
        vals_t[:, at] = kvs[at, HD : 2 * HD].T
        row = lax.broadcasted_iota(jnp.int32, (count, 1), 0)
        base = 0
        for index, block in enumerate(blocks_in(first, count)):
            base = jnp.where(row // BLOCK == index, device(*block) * BLOCK, base)
        key_pos = base + row % BLOCK
        logits = dot(kvs[at, 0:HD], queries[...], 1, 1) * (SCALE * LOG2E)
        logits = jnp.where(key_pos <= limit, logits, masked_score)
        score[at, :] = logits
        return fold8(logits, jnp.max)

    def widen(total, own, combine):
        return jnp.concatenate([combine(total[:, own_cols], own), total[:, ROLL_ROWS:]], axis=1)

    def weigh(at, cols, row_max):
        expo = jnp.exp2(score[at, cols] - row_max)
        rounded = expo.astype(BF16)
        weight[at, cols] = rounded
        return fold8(expo, jnp.sum), dot(vals_t[:, at], rounded, 1, 0)

    def grad_probs_of(at):
        return dot(kvs[at, HD : 2 * HD], grads[...], 1, 1)

    own_key = lax.broadcasted_iota(jnp.int32, (RESP, 1), 0)
    own_logits = dot(rkv[:, 0:HD], queries[own_cols, :], 1, 1) * (SCALE * LOG2E)
    own_logits = jnp.where(own_key <= own_limit, own_logits, masked_score)
    score[own_rows, own_cols] = own_logits
    own_max = fold8(own_logits, jnp.max)
    keys_t[:, own_rows] = rkv[:, 0:HD].T
    vals_t[:, own_rows] = rkv[:, HD : 2 * HD].T
    gradp[own_rows, own_cols] = dot(rkv[:, HD : 2 * HD], grads[own_cols, :], 1, 1)
    grad_t = grads[...].T.astype(F32)

    pair = CORES * BLOCK
    for place in (1, 3, 2):
        arrived(0, place, 0)
        relay_near(place)
    arrived(0, 0, 1)
    near_max = take(0, 2 * pair)

    @pl.when(my_core == 1)
    def _():
        for core in range(CORES):
            arrived(1, 0, core)
        for place in (2, 1, 3):
            for core in range(CORES):
                along_row(place, core)
        for core in range(CORES):
            to_sibling(0, core)

    for place in (1, 3, 2):
        arrived(0, place, 1)
    near_max = jnp.maximum(near_max, take(2 * pair, 2 * pair))
    near_max = widen(near_max, own_max, jnp.maximum)
    row_max = jnp.max(near_max, axis=0, keepdims=True)
    near = pl.ds(0, ROW * pair)
    row_sum, out_t = weigh(near, all_cols, row_max)
    own_sum_8, own_out = weigh(own_rows, own_cols, row_max[:, own_cols])
    row_sum = jnp.sum(widen(row_sum, own_sum_8, jnp.add), axis=0, keepdims=True)
    out_t = widen(out_t, own_out, jnp.add)
    phase_max = [row_max]
    gradp[near, :] = grad_probs_of(near)

    def fold_in(first, count, state):
        row_max, row_sum, out_t = state
        new_max = jnp.max(take(first, count), axis=0, keepdims=True)
        new_max = jnp.maximum(row_max, new_max)
        shrink = jnp.exp2(row_max - new_max)
        more_sum, more_out = weigh(pl.ds(first, count), all_cols, new_max)
        phase_max.append(new_max)
        row_sum = row_sum * shrink + jnp.sum(more_sum, axis=0, keepdims=True)
        return new_max, row_sum, out_t * shrink + more_out

    far = ROW * pair

    @pl.when(my_core == 0)
    def _():
        for core in range(CORES):
            arrived(1, 0, core)

    state = fold_in(far, pair, (row_max, row_sum, out_t))
    gradp[pl.ds(far, pair), :] = grad_probs_of(pl.ds(far, pair))
    def hear(*places):
        for place in places:
            for core in range(CORES):
                arrived(1, place, core)

        @pl.when(my_core == 1)
        def _():
            for place in places:
                for core in range(CORES):
                    to_sibling(place, core)

    hear(1, 3)
    state = fold_in(far + pair, 2 * pair, state)
    hear(2)
    row_max, row_sum, out_t = fold_in(far + 3 * pair, pair, state)

    inverse = jnp.where(rows_left > 0, 1.0 / row_sum, 0.0)
    out_t = (out_t * inverse).astype(BF16)
    row_dot = jnp.sum(grad_t * out_t.astype(F32), axis=0, keepdims=True)
    factors = [jnp.exp2(past - row_max) * inverse for past in phase_max]

    def back(at, cols, grad_probs, factor):
        probs = weight[at, cols].astype(F32) * factor[:, cols]
        grad_logits = (probs * (grad_probs - row_dot[:, cols])).astype(BF16)
        weight[at, cols] = grad_logits
        grad_vals = dot(probs.astype(BF16), grads[cols, :], 1, 0)
        grad_keys = dot(grad_logits, queries[cols, :], 1, 0) * SCALE
        return grad_keys, grad_vals

    def term_copy(source, target, sent, landed, to):
        return pltpu.make_async_remote_copy(
            src_ref=source,
            dst_ref=target,
            send_sem=sum_send_sem.at[sent],
            recv_sem=sum_recv_sem.at[landed],
            device_id={"roll": device(*to)},
            device_id_type=MESH,
        )

    def ship(source, target, index, to):
        copy = term_copy(source, target, index, index, to)
        copy.start()
        return copy

    sums = {}

    def prefix_back(first, count, grad_probs, factor):
        grad_keys, grad_vals = back(pl.ds(first, count), all_cols, grad_probs, factor)
        for index, (half, place, core) in enumerate(blocks_in(first, count)):
            at = half * ROW + POS[place]
            rows = slice(index * BLOCK, (index + 1) * BLOCK)
            if core == 0:
                own_sum[at, :, 0:HD] = grad_keys[rows]
                own_sum[at, :, HD : 2 * HD] = grad_vals[rows]
            else:
                to_core[at, :, 0:HD] = grad_keys[rows].astype(BF16)
                to_core[at, :, HD : 2 * HD] = grad_vals[rows].astype(BF16)
                sums["core", at] = ship(to_core.at[at], from_core.at[at], at, (0, 0, 1))

    def chip_total(at):
        sums["core", at].wait_recv()
        return own_sum[at] + from_core[at].astype(F32)

    def send_on(half, place, to):
        at = half * ROW + POS[place]
        to_owner[at] = chip_total(at).astype(BF16)
        lands = half * ROW + POS[(ROW - place) % ROW]
        sums["owner", lands] = ship(
            to_owner.at[at], from_owner.at[lands], HALVES * ROW + lands, to
        )

    def neighbour_copy(place):
        at = ROW + POS[place]
        first = (POS[ROW - place] - 1) * CORES
        return term_copy(
            to_owner.at[at],
            from_row.at[first + my_core],
            2 * HALVES * ROW + place,
            2 * HALVES * ROW + first + my_core,
            (0, place, speaker),
        )

    def neighbour_arrived(index):
        term_copy(
            from_row.at[index], from_row.at[index], 0, 2 * HALVES * ROW + index, (0, 0, 1)
        ).wait_recv()

    sibling_copy = term_copy(to_owner.at[ROW], from_row.at[4], 20, 20, (0, 0, 1))

    def opposite_copy(core):
        return term_copy(
            to_opposite.at[core],
            from_owner.at[ROW],
            21 + core,
            HALVES * ROW + ROW,
            (1, 0, (core + 1) % CORES),
        )

    last = pl.ds(far + 3 * pair, pair)
    cross = pl.ds(far + 2 * pair, pair)
    straight = pl.ds(far + pair, pair)
    prefix_back(far + 2 * pair, pair, grad_probs_of(cross), factors[2])
    prefix_back(far + 3 * pair, pair, grad_probs_of(last), factors[3])
    prefix_back(far + pair, pair, grad_probs_of(straight), factors[2])
    for place in (1, 3):
        at = ROW + POS[place]
        to_owner[at] = chip_total(at).astype(BF16)
        neighbour_copy(place).start()
    send_on(1, 2, (1, 2, 0))
    prefix_back(far, pair, gradp[pl.ds(far, pair), :], factors[1])
    prefix_back(2 * pair, 2 * pair, gradp[pl.ds(2 * pair, 2 * pair), :], factors[0])

    @pl.when(my_core == 0)
    def _():
        to_owner[ROW] = chip_total(ROW).astype(BF16)
        sibling_copy.start()

    prefix_back(0, 2 * pair, gradp[pl.ds(0, 2 * pair), :], factors[0])
    send_on(0, 2, (0, 2, 0))
    send_on(0, 3, (0, 3, 0))
    send_on(0, 1, (0, 1, 0))
    grad_keys, grad_vals = back(
        own_rows, own_cols, gradp[own_rows, own_cols], factors[0]
    )
    roll_dkv[0, :, 0:HD] = grad_keys.astype(BF16)
    roll_dkv[0, :, HD : 2 * HD] = grad_vals.astype(BF16)

    @pl.when(my_core == 1)
    def _():
        term = chip_total(ROW)
        for index in (1, 3):
            neighbour_arrived(index)
            term = term + from_row[index].astype(F32)
        to_opposite[1] = term.astype(BF16)
        opposite_copy(1).start()
        sibling_copy.wait_recv()
        term = from_row[4].astype(F32)
        for index in (0, 2):
            neighbour_arrived(index)
            term = term + from_row[index].astype(F32)
        to_opposite[0] = term.astype(BF16)
        opposite_copy(0).start()

    out = out_t.T
    for head in range(HEADS):
        columns = slice(head * HD, (head + 1) * HD)
        roll_out[0, :, columns] = out[head * RESP : (head + 1) * RESP]
        at = ROLL_ROWS + head * BLOCK
        pre_out[:, columns] = out[at : at + BLOCK]
    grad_query = dot(keys_t[:, 0:PREFIX], weight[0:PREFIX, :], 1, 0)
    grad_query = widen(
        grad_query, dot(keys_t[:, own_rows], weight[own_rows, own_cols], 1, 0), jnp.add
    )
    grad_query = (grad_query * SCALE).astype(BF16).T
    for head in range(HEADS):
        columns = slice(head * HD, (head + 1) * HD)
        roll_dq[0, :, columns] = grad_query[head * RESP : (head + 1) * RESP]
        at = ROLL_ROWS + head * BLOCK
        pre_dq[:, columns] = grad_query[at : at + BLOCK]

    total = chip_total(0)
    for at in (1, 2, 3, ROW + POS[2]):
        sums["owner", at].wait_recv()
        total = total + from_owner[at].astype(F32)
    opposite_copy(0).wait_recv()
    pre_dkv[...] = (total + from_owner[ROW].astype(F32)).astype(BF16)
    for copy in (*copies, *sums.values(), neighbour_copy(1), neighbour_copy(3)):
        copy.wait_send()

    @pl.when(my_core == 0)
    def _():
        sibling_copy.wait_send()

    @pl.when(my_core == 1)
    def _():
        for core in range(CORES):
            opposite_copy(core).wait_send()
            for place in (1, 2, 3):
                along_row(place, core, start=False)
            for place in range(ROW):
                to_sibling(place, core, start=False)


def drain(*refs):
    count = (len(refs) - 1) // 2
    sem = refs[-1]
    copies = [
        pltpu.make_async_copy(refs[index], refs[count + index], sem.at[index])
        for index in range(count)
    ]
    for copy in copies:
        copy.start()
    for copy in copies:
        copy.wait()


def on_device(pre_q, pre_kv, roll_q, roll_kv, pre_grad, roll_grad, pre_len, roll_len):
    smem = pl.BlockSpec(memory_space=pltpu.SMEM)
    vmem = pl.BlockSpec(memory_space=pltpu.VMEM)
    anywhere = pl.BlockSpec(memory_space=pl.ANY)
    like = lambda array: pltpu.VMEM(array.shape, BF16)
    final = lambda array: jax.ShapeDtypeStruct(array.shape, BF16)
    copies = 2 * GROUP
    sums = 24
    results = pl.pallas_call(
        kernel,
        out_shape=(
            like(pre_q),
            like(roll_q),
            like(pre_q),
            like(roll_q),
            like(pre_kv),
            like(roll_kv),
        ),
        in_specs=[smem] * 2 + [anywhere] * 6,
        out_specs=[vmem] * 6,
        scratch_shapes=[
            pltpu.VMEM((RESP, HEADS * HD), BF16),
            pltpu.VMEM((RESP, HEADS * HD), BF16),
            pltpu.VMEM((BLOCK, HEADS * HD), BF16),
            pltpu.VMEM((BLOCK, HEADS * HD), BF16),
            pltpu.VMEM((RESP, 2 * HD), BF16),
            pltpu.VMEM((PREFIX, 2 * HD), BF16),
            pltpu.VMEM((ROWS, HD), BF16),
            pltpu.VMEM((ROWS, HD), BF16),
            pltpu.VMEM((PREFIX + RESP, ROWS), F32),
            pltpu.VMEM((PREFIX + RESP, ROWS), BF16),
            pltpu.VMEM((PREFIX + RESP, ROWS), F32),
            pltpu.VMEM((HD, PREFIX + RESP), BF16),
            pltpu.VMEM((HD, PREFIX + RESP), BF16),
            pltpu.VMEM((HALVES * ROW, BLOCK, 2 * HD), BF16),
            pltpu.VMEM((HALVES * ROW, BLOCK, 2 * HD), BF16),
            pltpu.VMEM((HALVES * ROW, BLOCK, 2 * HD), F32),
            pltpu.VMEM((HALVES * ROW, BLOCK, 2 * HD), BF16),
            pltpu.VMEM((HALVES * ROW, BLOCK, 2 * HD), BF16),
            pltpu.VMEM((5, BLOCK, 2 * HD), BF16),
            pltpu.VMEM((CORES, BLOCK, 2 * HD), BF16),
            pltpu.SemaphoreType.DMA((6,)),
            pltpu.SemaphoreType.DMA((copies,)),
            pltpu.SemaphoreType.DMA((copies,)),
            pltpu.SemaphoreType.DMA((sums,)),
            pltpu.SemaphoreType.DMA((sums,)),
        ],
        compiler_params=pltpu.CompilerParams(
            collective_id=0, has_side_effects=True, vmem_limit_bytes=56 << 20
        ),
    )(pre_len, roll_len, pre_q, pre_kv, roll_q, roll_kv, pre_grad, roll_grad)
    return pl.pallas_call(
        drain,
        out_shape=tuple(final(array) for array in (pre_q, roll_q, pre_q, roll_q, pre_kv, roll_kv)),
        in_specs=[vmem] * 6,
        out_specs=[anywhere] * 6,
        scratch_shapes=[pltpu.SemaphoreType.DMA((6,))],
    )(*(pltpu.with_memory_space_constraint(result, pltpu.VMEM) for result in results))


def solution(mesh):
    in_specs = (
        P(("prompt", "roll"), None),
        P(("prompt", "roll"), None),
        P(("prompt", "roll"), None, None),
        P(("prompt", "roll"), None, None),
        P(("prompt", "roll"), None),
        P(("prompt", "roll"), None, None),
        P("prompt"),
        P(("prompt", "roll")),
    )
    out_specs = (
        P(("prompt", "roll"), None),
        P(("prompt", "roll"), None, None),
        P(("prompt", "roll"), None),
        P(("prompt", "roll"), None, None),
        P(("prompt", "roll"), None),
        P(("prompt", "roll"), None, None),
    )
    return jax.shard_map(
        on_device, mesh=mesh, in_specs=in_specs, out_specs=out_specs, check_vma=False
    )
```

```python
import functools

import jax
import jax.numpy as jnp
from jax import lax
from jax.experimental import pallas as pl
from jax.experimental.pallas import tpu as pltpu
from jax.sharding import PartitionSpec as P

F32 = jnp.float32
BF16 = jnp.bfloat16
MESH = pl.DeviceIdType.MESH
masked_score = -1e30
HALVES, ROW, CORES = 2, 4, 2
BLOCK = 64
RESP = 128
HEADS = 8
HD = 128
GROUP = HALVES * ROW * CORES
PREFIX = GROUP * BLOCK
ROLL_ROWS = HEADS * RESP
ROWS = HEADS * (RESP + BLOCK)
SCALE = HD**-0.5
LOG2E = 1.4426950408889634


def dot(left, right, left_dim, right_dim):
    return lax.dot_general(
        left, right, (((left_dim,), (right_dim,)), ((), ())), preferred_element_type=F32
    )


POS = (0, 1, 3, 2)
LAYOUT = ((0, 0), (0, 1), (1, 0), (3, 0), (1, 1), (3, 1), (2, 0), (2, 1))


def slot(half, place, core):
    return half * len(LAYOUT) + LAYOUT.index((place, core))


def blocks_in(first, count):
    slots = range(first // BLOCK, (first + count) // BLOCK)
    return [(at // len(LAYOUT), *LAYOUT[at % len(LAYOUT)]) for at in slots]


def rows_of(half, place, core):
    return pl.ds(slot(half, place, core) * BLOCK, BLOCK)


def fold8(values, combine):
    return combine(values.reshape(values.shape[0] // 8, 8, values.shape[1]), axis=0)


def kernel(
    pre_len_ref,
    roll_len_ref,
    pre_q,
    pre_kv,
    roll_q,
    roll_kv,
    pre_grad,
    roll_grad,
    pre_out,
    roll_out,
    pre_dq,
    roll_dq,
    pre_dkv,
    roll_dkv,
    rq,
    rg,
    pq,
    pg,
    rkv,
    kvs,
    queries,
    grads,
    score,
    weight,
    gradp,
    keys_t,
    vals_t,
    to_core,
    from_core,
    own_sum,
    to_owner,
    from_owner,
    from_row,
    to_opposite,
    load_sem,
    send_sem,
    recv_sem,
    sum_send_sem,
    sum_recv_sem,
):
    me = lax.axis_index("roll")
    my_half, my_place, my_core = me // (ROW * CORES), (me // CORES) % ROW, me % CORES

    def device(half, place, core):
        return (
            ((my_half + half) % HALVES) * (ROW * CORES)
            + ((my_place + place) % ROW) * CORES
            + (my_core + core) % CORES
        )

    speaker = 1 - my_core
    partners = [(0, 0, 1), (0, 1, 0), (0, 3, 0), (0, 2, 0)]
    barrier = pltpu.get_barrier_semaphore()

    def announce(partner):
        pl.semaphore_signal(
            barrier, inc=1, device_id={"roll": device(*partner)}, device_id_type=MESH
        )

    @pl.when(my_core == 1)
    def _():
        announce((1, 0, 0))
        announce((1, 0, 1))

    for partner in partners:
        announce(partner)

    loads = []
    for index, (source, target) in enumerate(
        (
            (pre_kv, kvs.at[rows_of(0, 0, 0)]),
            (roll_kv.at[0], rkv),
            (roll_q.at[0], rq),
            (pre_q, pq),
            (roll_grad.at[0], rg),
            (pre_grad, pg),
        )
    ):
        loads.append(pltpu.make_async_copy(source, target, load_sem.at[index]))
        loads[-1].start()

    def block_copy(source, at, index, to):
        return pltpu.make_async_remote_copy(
            src_ref=source,
            dst_ref=kvs.at[pl.ds(at * BLOCK, BLOCK)],
            send_sem=send_sem.at[index],
            recv_sem=recv_sem.at[at],
            device_id={"roll": device(*to)},
            device_id_type=MESH,
        )

    def push(source, at, index, to):
        copy = block_copy(source, at, index, to)
        copy.start()
        return copy

    def arrived(*block):
        at = slot(*block)
        block_copy(kvs.at[rows_of(*block)], at, 0, (0, 0, 1)).wait_recv()

    def relay_near(place):
        at = slot(0, place, 1)
        copies.append(push(kvs.at[rows_of(0, place, 0)], at, at, (0, 0, 1)))

    def to_sibling(place, core, start=True):
        at = slot(1, place, 1 - core)
        copy = block_copy(kvs.at[rows_of(1, place, core)], at, GROUP + at, (0, 0, 1))
        copy.start() if start else copy.wait_send()

    def along_row(place, core, start=True):
        at = slot(1, ROW - place, core)
        copy = block_copy(kvs.at[rows_of(1, 0, core)], at, GROUP + place * CORES + core, (0, place, 0))
        copy.start() if start else copy.wait_send()

    copies = []
    loads[0].wait()
    pl.semaphore_wait(barrier, len(partners) + 1)
    held = kvs.at[rows_of(0, 0, 0)]
    copies.append(push(held, slot(1, 0, 0) + speaker, 0, (1, 0, speaker)))
    for place in (2, 1, 3):
        at = slot(0, ROW - place, 0)
        copies.append(push(held, at, at, (0, place, 0)))
    at = slot(0, 0, 1)
    copies.append(push(held, at, at, (0, 0, 1)))

    pre_len = pre_len_ref[0]
    roll_len = roll_len_ref[0]
    lane = lax.broadcasted_iota(jnp.int32, (1, ROWS), 1)
    is_roll = lane < ROLL_ROWS
    query_pos = me * BLOCK + lane % BLOCK
    limit = jnp.where(is_roll, pre_len - 1, jnp.minimum(query_pos, pre_len - 1))
    own_limit = jnp.minimum(lane[:, :ROLL_ROWS] % RESP, roll_len - 1)
    rows_left = jnp.where(is_roll, roll_len - lane % RESP, pre_len - query_pos)

    for load in loads[1:]:
        load.wait()
    for head in range(HEADS):
        columns = slice(head * HD, (head + 1) * HD)
        at = pl.ds(head * RESP, RESP)
        queries[at, :] = rq[:, columns]
        grads[at, :] = rg[:, columns]
        at = pl.ds(ROLL_ROWS + head * BLOCK, BLOCK)
        queries[at, :] = pq[:, columns]
        grads[at, :] = pg[:, columns]

    own_rows = pl.ds(PREFIX, RESP)
    all_cols = slice(0, ROWS)
    own_cols = slice(0, ROLL_ROWS)

    def take(first, count):
        at = pl.ds(first, count)
        keys_t[:, at] = kvs[at, 0:HD].T
        vals_t[:, at] = kvs[at, HD : 2 * HD].T
        row = lax.broadcasted_iota(jnp.int32, (count, 1), 0)
        base = 0
        for index, block in enumerate(blocks_in(first, count)):
            base = jnp.where(row // BLOCK == index, device(*block) * BLOCK, base)
        key_pos = base + row % BLOCK
        logits = dot(kvs[at, 0:HD], queries[...], 1, 1) * (SCALE * LOG2E)
        logits = jnp.where(key_pos <= limit, logits, masked_score)
        score[at, :] = logits
        return fold8(logits, jnp.max)

    def widen(total, own, combine):
        return jnp.concatenate([combine(total[:, own_cols], own), total[:, ROLL_ROWS:]], axis=1)

    def weigh(at, cols, row_max):
        expo = jnp.exp2(score[at, cols] - row_max)
        rounded = expo.astype(BF16)
        weight[at, cols] = rounded
        return fold8(expo, jnp.sum), dot(vals_t[:, at], rounded, 1, 0)

    def grad_probs_of(at):
        return dot(kvs[at, HD : 2 * HD], grads[...], 1, 1)

    own_key = lax.broadcasted_iota(jnp.int32, (RESP, 1), 0)
    own_logits = dot(rkv[:, 0:HD], queries[own_cols, :], 1, 1) * (SCALE * LOG2E)
    own_logits = jnp.where(own_key <= own_limit, own_logits, masked_score)
    score[own_rows, own_cols] = own_logits
    own_max = fold8(own_logits, jnp.max)
    keys_t[:, own_rows] = rkv[:, 0:HD].T
    vals_t[:, own_rows] = rkv[:, HD : 2 * HD].T
    gradp[own_rows, own_cols] = dot(rkv[:, HD : 2 * HD], grads[own_cols, :], 1, 1)
    grad_t = grads[...].T.astype(F32)

    pair = CORES * BLOCK
    for place in (1, 3, 2):
        arrived(0, place, 0)
        relay_near(place)
    arrived(0, 0, 1)
    near_max = take(0, 2 * pair)

    @pl.when(my_core == 1)
    def _():
        for core in range(CORES):
            arrived(1, 0, core)
        for core in range(CORES):
            to_sibling(0, core)
        for place in (1, 3, 2):
            for core in range(CORES):
                along_row(place, core)

    for place in (1, 3, 2):
        arrived(0, place, 1)
    near_max = jnp.maximum(near_max, take(2 * pair, 2 * pair))
    near_max = widen(near_max, own_max, jnp.maximum)
    row_max = jnp.max(near_max, axis=0, keepdims=True)
    near = pl.ds(0, ROW * pair)
    row_sum, out_t = weigh(near, all_cols, row_max)
    own_sum_8, own_out = weigh(own_rows, own_cols, row_max[:, own_cols])
    row_sum = jnp.sum(widen(row_sum, own_sum_8, jnp.add), axis=0, keepdims=True)
    out_t = widen(out_t, own_out, jnp.add)
    phase_max = [row_max]
    gradp[near, :] = grad_probs_of(near)

    def fold_in(first, count, state):
        row_max, row_sum, out_t = state
        new_max = jnp.max(take(first, count), axis=0, keepdims=True)
        new_max = jnp.maximum(row_max, new_max)
        shrink = jnp.exp2(row_max - new_max)
        more_sum, more_out = weigh(pl.ds(first, count), all_cols, new_max)
        phase_max.append(new_max)
        row_sum = row_sum * shrink + jnp.sum(more_sum, axis=0, keepdims=True)
        return new_max, row_sum, out_t * shrink + more_out

    far = ROW * pair

    @pl.when(my_core == 0)
    def _():
        for core in range(CORES):
            arrived(1, 0, core)

    state = fold_in(far, pair, (row_max, row_sum, out_t))
    gradp[pl.ds(far, pair), :] = grad_probs_of(pl.ds(far, pair))
    def hear(*places):
        for place in places:
            for core in range(CORES):
                arrived(1, place, core)

        @pl.when(my_core == 1)
        def _():
            for place in places:
                for core in range(CORES):
                    to_sibling(place, core)

    hear(1, 3)
    state = fold_in(far + pair, 2 * pair, state)
    hear(2)
    row_max, row_sum, out_t = fold_in(far + 3 * pair, pair, state)

    inverse = jnp.where(rows_left > 0, 1.0 / row_sum, 0.0)
    out_t = (out_t * inverse).astype(BF16)
    row_dot = jnp.sum(grad_t * out_t.astype(F32), axis=0, keepdims=True)
    factors = [jnp.exp2(past - row_max) * inverse for past in phase_max]

    def back(at, cols, grad_probs, factor):
        probs = weight[at, cols].astype(F32) * factor[:, cols]
        grad_logits = (probs * (grad_probs - row_dot[:, cols])).astype(BF16)
        weight[at, cols] = grad_logits
        grad_vals = dot(probs.astype(BF16), grads[cols, :], 1, 0)
        grad_keys = dot(grad_logits, queries[cols, :], 1, 0) * SCALE
        return grad_keys, grad_vals

    def term_copy(source, target, sent, landed, to):
        return pltpu.make_async_remote_copy(
            src_ref=source,
            dst_ref=target,
            send_sem=sum_send_sem.at[sent],
            recv_sem=sum_recv_sem.at[landed],
            device_id={"roll": device(*to)},
            device_id_type=MESH,
        )

    def ship(source, target, index, to):
        copy = term_copy(source, target, index, index, to)
        copy.start()
        return copy

    sums = {}

    def prefix_back(first, count, grad_probs, factor):
        grad_keys, grad_vals = back(pl.ds(first, count), all_cols, grad_probs, factor)
        for index, (half, place, core) in enumerate(blocks_in(first, count)):
            at = half * ROW + POS[place]
            rows = slice(index * BLOCK, (index + 1) * BLOCK)
            if core == 0:
                own_sum[at, :, 0:HD] = grad_keys[rows]
                own_sum[at, :, HD : 2 * HD] = grad_vals[rows]
            else:
                to_core[at, :, 0:HD] = grad_keys[rows].astype(BF16)
                to_core[at, :, HD : 2 * HD] = grad_vals[rows].astype(BF16)
                sums["core", at] = ship(to_core.at[at], from_core.at[at], at, (0, 0, 1))

    def chip_total(at):
        sums["core", at].wait_recv()
        return own_sum[at] + from_core[at].astype(F32)

    def send_on(half, place, to):
        at = half * ROW + POS[place]
        to_owner[at] = chip_total(at).astype(BF16)
        lands = half * ROW + POS[(ROW - place) % ROW]
        sums["owner", lands] = ship(
            to_owner.at[at], from_owner.at[lands], HALVES * ROW + lands, to
        )

    def neighbour_copy(place):
        at = ROW + POS[place]
        first = (POS[ROW - place] - 1) * CORES
        return term_copy(
            to_owner.at[at],
            from_row.at[first + my_core],
            2 * HALVES * ROW + place,
            2 * HALVES * ROW + first + my_core,
            (0, place, speaker),
        )

    def neighbour_arrived(index):
        term_copy(
            from_row.at[index], from_row.at[index], 0, 2 * HALVES * ROW + index, (0, 0, 1)
        ).wait_recv()

    sibling_copy = term_copy(to_owner.at[ROW], from_row.at[4], 20, 20, (0, 0, 1))

    def opposite_copy(core):
        return term_copy(
            to_opposite.at[core],
            from_owner.at[ROW],
            21 + core,
            HALVES * ROW + ROW,
            (1, 0, (core + 1) % CORES),
        )

    last = pl.ds(far + 3 * pair, pair)
    cross = pl.ds(far + 2 * pair, pair)
    straight = pl.ds(far + pair, pair)
    prefix_back(far + 2 * pair, pair, grad_probs_of(cross), factors[2])
    prefix_back(far + 3 * pair, pair, grad_probs_of(last), factors[3])
    prefix_back(far + pair, pair, grad_probs_of(straight), factors[2])
    for place in (1, 3):
        at = ROW + POS[place]
        to_owner[at] = chip_total(at).astype(BF16)
        neighbour_copy(place).start()
    send_on(1, 2, (1, 2, 0))
    prefix_back(far, pair, gradp[pl.ds(far, pair), :], factors[1])
    prefix_back(2 * pair, 2 * pair, gradp[pl.ds(2 * pair, 2 * pair), :], factors[0])

    @pl.when(my_core == 0)
    def _():
        to_owner[ROW] = chip_total(ROW).astype(BF16)
        sibling_copy.start()

    prefix_back(0, 2 * pair, gradp[pl.ds(0, 2 * pair), :], factors[0])
    send_on(0, 2, (0, 2, 0))
    send_on(0, 3, (0, 3, 0))
    send_on(0, 1, (0, 1, 0))
    grad_keys, grad_vals = back(
        own_rows, own_cols, gradp[own_rows, own_cols], factors[0]
    )
    roll_dkv[0, :, 0:HD] = grad_keys.astype(BF16)
    roll_dkv[0, :, HD : 2 * HD] = grad_vals.astype(BF16)

    @pl.when(my_core == 1)
    def _():
        term = chip_total(ROW)
        for index in (1, 3):
            neighbour_arrived(index)
            term = term + from_row[index].astype(F32)
        to_opposite[1] = term.astype(BF16)
        opposite_copy(1).start()
        sibling_copy.wait_recv()
        term = from_row[4].astype(F32)
        for index in (0, 2):
            neighbour_arrived(index)
            term = term + from_row[index].astype(F32)
        to_opposite[0] = term.astype(BF16)
        opposite_copy(0).start()

    out = out_t.T
    for head in range(HEADS):
        columns = slice(head * HD, (head + 1) * HD)
        roll_out[0, :, columns] = out[head * RESP : (head + 1) * RESP]
        at = ROLL_ROWS + head * BLOCK
        pre_out[:, columns] = out[at : at + BLOCK]
    grad_query = dot(keys_t[:, 0:PREFIX], weight[0:PREFIX, :], 1, 0)
    grad_query = widen(
        grad_query, dot(keys_t[:, own_rows], weight[own_rows, own_cols], 1, 0), jnp.add
    )
    grad_query = (grad_query * SCALE).astype(BF16).T
    for head in range(HEADS):
        columns = slice(head * HD, (head + 1) * HD)
        roll_dq[0, :, columns] = grad_query[head * RESP : (head + 1) * RESP]
        at = ROLL_ROWS + head * BLOCK
        pre_dq[:, columns] = grad_query[at : at + BLOCK]

    total = chip_total(0)
    for at in (1, 2, 3, ROW + POS[2]):
        sums["owner", at].wait_recv()
        total = total + from_owner[at].astype(F32)
    opposite_copy(0).wait_recv()
    pre_dkv[...] = (total + from_owner[ROW].astype(F32)).astype(BF16)
    for copy in (*copies, *sums.values(), neighbour_copy(1), neighbour_copy(3)):
        copy.wait_send()

    @pl.when(my_core == 0)
    def _():
        sibling_copy.wait_send()

    @pl.when(my_core == 1)
    def _():
        for core in range(CORES):
            opposite_copy(core).wait_send()
            for place in (1, 2, 3):
                along_row(place, core, start=False)
            for place in range(ROW):
                to_sibling(place, core, start=False)


def drain(*refs):
    count = (len(refs) - 1) // 2
    sem = refs[-1]
    copies = [
        pltpu.make_async_copy(refs[index], refs[count + index], sem.at[index])
        for index in range(count)
    ]
    for copy in copies:
        copy.start()
    for copy in copies:
        copy.wait()


def on_device(pre_q, pre_kv, roll_q, roll_kv, pre_grad, roll_grad, pre_len, roll_len):
    smem = pl.BlockSpec(memory_space=pltpu.SMEM)
    vmem = pl.BlockSpec(memory_space=pltpu.VMEM)
    anywhere = pl.BlockSpec(memory_space=pl.ANY)
    like = lambda array: pltpu.VMEM(array.shape, BF16)
    final = lambda array: jax.ShapeDtypeStruct(array.shape, BF16)
    copies = 2 * GROUP
    sums = 24
    results = pl.pallas_call(
        kernel,
        out_shape=(
            like(pre_q),
            like(roll_q),
            like(pre_q),
            like(roll_q),
            like(pre_kv),
            like(roll_kv),
        ),
        in_specs=[smem] * 2 + [anywhere] * 6,
        out_specs=[vmem] * 6,
        scratch_shapes=[
            pltpu.VMEM((RESP, HEADS * HD), BF16),
            pltpu.VMEM((RESP, HEADS * HD), BF16),
            pltpu.VMEM((BLOCK, HEADS * HD), BF16),
            pltpu.VMEM((BLOCK, HEADS * HD), BF16),
            pltpu.VMEM((RESP, 2 * HD), BF16),
            pltpu.VMEM((PREFIX, 2 * HD), BF16),
            pltpu.VMEM((ROWS, HD), BF16),
            pltpu.VMEM((ROWS, HD), BF16),
            pltpu.VMEM((PREFIX + RESP, ROWS), F32),
            pltpu.VMEM((PREFIX + RESP, ROWS), BF16),
            pltpu.VMEM((PREFIX + RESP, ROWS), F32),
            pltpu.VMEM((HD, PREFIX + RESP), BF16),
            pltpu.VMEM((HD, PREFIX + RESP), BF16),
            pltpu.VMEM((HALVES * ROW, BLOCK, 2 * HD), BF16),
            pltpu.VMEM((HALVES * ROW, BLOCK, 2 * HD), BF16),
            pltpu.VMEM((HALVES * ROW, BLOCK, 2 * HD), F32),
            pltpu.VMEM((HALVES * ROW, BLOCK, 2 * HD), BF16),
            pltpu.VMEM((HALVES * ROW, BLOCK, 2 * HD), BF16),
            pltpu.VMEM((5, BLOCK, 2 * HD), BF16),
            pltpu.VMEM((CORES, BLOCK, 2 * HD), BF16),
            pltpu.SemaphoreType.DMA((6,)),
            pltpu.SemaphoreType.DMA((copies,)),
            pltpu.SemaphoreType.DMA((copies,)),
            pltpu.SemaphoreType.DMA((sums,)),
            pltpu.SemaphoreType.DMA((sums,)),
        ],
        compiler_params=pltpu.CompilerParams(
            collective_id=0, has_side_effects=True, vmem_limit_bytes=56 << 20
        ),
    )(pre_len, roll_len, pre_q, pre_kv, roll_q, roll_kv, pre_grad, roll_grad)
    return pl.pallas_call(
        drain,
        out_shape=tuple(final(array) for array in (pre_q, roll_q, pre_q, roll_q, pre_kv, roll_kv)),
        in_specs=[vmem] * 6,
        out_specs=[anywhere] * 6,
        scratch_shapes=[pltpu.SemaphoreType.DMA((6,))],
    )(*(pltpu.with_memory_space_constraint(result, pltpu.VMEM) for result in results))


def solution(mesh):
    in_specs = (
        P(("prompt", "roll"), None),
        P(("prompt", "roll"), None),
        P(("prompt", "roll"), None, None),
        P(("prompt", "roll"), None, None),
        P(("prompt", "roll"), None),
        P(("prompt", "roll"), None, None),
        P("prompt"),
        P(("prompt", "roll")),
    )
    out_specs = (
        P(("prompt", "roll"), None),
        P(("prompt", "roll"), None, None),
        P(("prompt", "roll"), None),
        P(("prompt", "roll"), None, None),
        P(("prompt", "roll"), None),
        P(("prompt", "roll"), None, None),
    )
    return jax.shard_map(
        on_device, mesh=mesh, in_specs=in_specs, out_specs=out_specs, check_vma=False
    )
```

```python
import functools

import jax
import jax.numpy as jnp
from jax import lax
from jax.experimental import pallas as pl
from jax.experimental.pallas import tpu as pltpu
from jax.sharding import PartitionSpec as P

F32 = jnp.float32
BF16 = jnp.bfloat16
MESH = pl.DeviceIdType.MESH
masked_score = -1e30
HALVES, ROW, CORES = 2, 4, 2
BLOCK = 64
RESP = 128
HEADS = 8
HD = 128
GROUP = HALVES * ROW * CORES
PREFIX = GROUP * BLOCK
ROLL_ROWS = HEADS * RESP
ROWS = HEADS * (RESP + BLOCK)
SCALE = HD**-0.5
LOG2E = 1.4426950408889634


def dot(left, right, left_dim, right_dim):
    return lax.dot_general(
        left, right, (((left_dim,), (right_dim,)), ((), ())), preferred_element_type=F32
    )


POS = (0, 1, 3, 2)
LAYOUT = ((0, 0), (0, 1), (1, 0), (3, 0), (1, 1), (3, 1), (2, 0), (2, 1))


def slot(half, place, core):
    return half * len(LAYOUT) + LAYOUT.index((place, core))


def blocks_in(first, count):
    slots = range(first // BLOCK, (first + count) // BLOCK)
    return [(at // len(LAYOUT), *LAYOUT[at % len(LAYOUT)]) for at in slots]


def rows_of(half, place, core):
    return pl.ds(slot(half, place, core) * BLOCK, BLOCK)


def fold8(values, combine):
    return combine(values.reshape(values.shape[0] // 8, 8, values.shape[1]), axis=0)


def kernel(
    pre_len_ref,
    roll_len_ref,
    pre_q,
    pre_kv,
    roll_q,
    roll_kv,
    pre_grad,
    roll_grad,
    pre_out,
    roll_out,
    pre_dq,
    roll_dq,
    pre_dkv,
    roll_dkv,
    rq,
    rg,
    pq,
    pg,
    rkv,
    kvs,
    queries,
    grads,
    score,
    weight,
    gradp,
    keys_t,
    vals_t,
    to_core,
    from_core,
    own_sum,
    to_owner,
    from_owner,
    from_row,
    to_opposite,
    load_sem,
    send_sem,
    recv_sem,
    sum_send_sem,
    sum_recv_sem,
):
    me = lax.axis_index("roll")
    my_half, my_place, my_core = me // (ROW * CORES), (me // CORES) % ROW, me % CORES

    def device(half, place, core):
        return (
            ((my_half + half) % HALVES) * (ROW * CORES)
            + ((my_place + place) % ROW) * CORES
            + (my_core + core) % CORES
        )

    speaker = 1 - my_core
    partners = [(0, 0, 1), (0, 1, 0), (0, 3, 0), (0, 2, 0)]
    barrier = pltpu.get_barrier_semaphore()

    def announce(partner):
        pl.semaphore_signal(
            barrier, inc=1, device_id={"roll": device(*partner)}, device_id_type=MESH
        )

    @pl.when(my_core == 1)
    def _():
        announce((1, 0, 0))
        announce((1, 0, 1))

    for partner in partners:
        announce(partner)

    loads = []
    for index, (source, target) in enumerate(
        (
            (pre_kv, kvs.at[rows_of(0, 0, 0)]),
            (roll_kv.at[0], rkv),
            (roll_q.at[0], rq),
            (pre_q, pq),
            (roll_grad.at[0], rg),
            (pre_grad, pg),
        )
    ):
        loads.append(pltpu.make_async_copy(source, target, load_sem.at[index]))
        loads[-1].start()

    def block_copy(source, at, index, to):
        return pltpu.make_async_remote_copy(
            src_ref=source,
            dst_ref=kvs.at[pl.ds(at * BLOCK, BLOCK)],
            send_sem=send_sem.at[index],
            recv_sem=recv_sem.at[at],
            device_id={"roll": device(*to)},
            device_id_type=MESH,
        )

    def push(source, at, index, to):
        copy = block_copy(source, at, index, to)
        copy.start()
        return copy

    def arrived(*block):
        at = slot(*block)
        block_copy(kvs.at[rows_of(*block)], at, 0, (0, 0, 1)).wait_recv()

    def relay_near(place):
        at = slot(0, place, 1)
        copies.append(push(kvs.at[rows_of(0, place, 0)], at, at, (0, 0, 1)))

    def to_sibling(place, core, start=True):
        at = slot(1, place, 1 - core)
        copy = block_copy(kvs.at[rows_of(1, place, core)], at, GROUP + at, (0, 0, 1))
        copy.start() if start else copy.wait_send()

    def along_row(place, core, start=True):
        at = slot(1, ROW - place, core)
        copy = block_copy(kvs.at[rows_of(1, 0, core)], at, GROUP + place * CORES + core, (0, place, 0))
        copy.start() if start else copy.wait_send()

    copies = []
    loads[0].wait()
    pl.semaphore_wait(barrier, len(partners) + 1)
    held = kvs.at[rows_of(0, 0, 0)]
    copies.append(push(held, slot(1, 0, 0) + speaker, 0, (1, 0, speaker)))
    for place in (2, 1, 3):
        at = slot(0, ROW - place, 0)
        copies.append(push(held, at, at, (0, place, 0)))
    at = slot(0, 0, 1)
    copies.append(push(held, at, at, (0, 0, 1)))

    pre_len = pre_len_ref[0]
    roll_len = roll_len_ref[0]
    lane = lax.broadcasted_iota(jnp.int32, (1, ROWS), 1)
    is_roll = lane < ROLL_ROWS
    query_pos = me * BLOCK + lane % BLOCK
    limit = jnp.where(is_roll, pre_len - 1, jnp.minimum(query_pos, pre_len - 1))
    own_limit = jnp.minimum(lane[:, :ROLL_ROWS] % RESP, roll_len - 1)
    rows_left = jnp.where(is_roll, roll_len - lane % RESP, pre_len - query_pos)

    for load in loads[1:]:
        load.wait()
    for head in range(HEADS):
        columns = slice(head * HD, (head + 1) * HD)
        at = pl.ds(head * RESP, RESP)
        queries[at, :] = rq[:, columns]
        grads[at, :] = rg[:, columns]
        at = pl.ds(ROLL_ROWS + head * BLOCK, BLOCK)
        queries[at, :] = pq[:, columns]
        grads[at, :] = pg[:, columns]

    own_rows = pl.ds(PREFIX, RESP)
    all_cols = slice(0, ROWS)
    own_cols = slice(0, ROLL_ROWS)

    def take(first, count):
        at = pl.ds(first, count)
        vals_t[:, at] = kvs[at, HD : 2 * HD].T
        row = lax.broadcasted_iota(jnp.int32, (count, 1), 0)
        base = 0
        for index, block in enumerate(blocks_in(first, count)):
            base = jnp.where(row // BLOCK == index, device(*block) * BLOCK, base)
        key_pos = base + row % BLOCK
        logits = dot(kvs[at, 0:HD], queries[...], 1, 1) * (SCALE * LOG2E)
        logits = jnp.where(key_pos <= limit, logits, masked_score)
        score[at, :] = logits
        return fold8(logits, jnp.max)

    def widen(total, own, combine):
        return jnp.concatenate([combine(total[:, own_cols], own), total[:, ROLL_ROWS:]], axis=1)

    def weigh(at, cols, row_max):
        expo = jnp.exp2(score[at, cols] - row_max)
        rounded = expo.astype(BF16)
        weight[at, cols] = rounded
        return fold8(expo, jnp.sum), dot(vals_t[:, at], rounded, 1, 0)

    def grad_probs_of(at):
        return dot(kvs[at, HD : 2 * HD], grads[...], 1, 1)

    own_key = lax.broadcasted_iota(jnp.int32, (RESP, 1), 0)
    own_logits = dot(rkv[:, 0:HD], queries[own_cols, :], 1, 1) * (SCALE * LOG2E)
    own_logits = jnp.where(own_key <= own_limit, own_logits, masked_score)
    score[own_rows, own_cols] = own_logits
    own_max = fold8(own_logits, jnp.max)
    vals_t[:, own_rows] = rkv[:, HD : 2 * HD].T
    gradp[own_rows, own_cols] = dot(rkv[:, HD : 2 * HD], grads[own_cols, :], 1, 1)
    grad_t = grads[...].T.astype(F32)

    pair = CORES * BLOCK
    for place in (1, 3, 2):
        arrived(0, place, 0)
        relay_near(place)
    arrived(0, 0, 1)
    near_max = take(0, 2 * pair)

    @pl.when(my_core == 1)
    def _():
        for core in range(CORES):
            arrived(1, 0, core)
        for core in range(CORES):
            to_sibling(0, core)
        for place in (1, 3, 2):
            for core in range(CORES):
                along_row(place, core)

    for place in (1, 3, 2):
        arrived(0, place, 1)
    near_max = jnp.maximum(near_max, take(2 * pair, 2 * pair))
    near_max = widen(near_max, own_max, jnp.maximum)
    row_max = jnp.max(near_max, axis=0, keepdims=True)
    near = pl.ds(0, ROW * pair)
    row_sum, out_t = weigh(near, all_cols, row_max)
    own_sum_8, own_out = weigh(own_rows, own_cols, row_max[:, own_cols])
    row_sum = jnp.sum(widen(row_sum, own_sum_8, jnp.add), axis=0, keepdims=True)
    out_t = widen(out_t, own_out, jnp.add)
    phase_max = [row_max]
    gradp[near, :] = grad_probs_of(near)

    def fold_in(first, count, state):
        row_max, row_sum, out_t = state
        new_max = jnp.max(take(first, count), axis=0, keepdims=True)
        new_max = jnp.maximum(row_max, new_max)
        shrink = jnp.exp2(row_max - new_max)
        more_sum, more_out = weigh(pl.ds(first, count), all_cols, new_max)
        phase_max.append(new_max)
        row_sum = row_sum * shrink + jnp.sum(more_sum, axis=0, keepdims=True)
        return new_max, row_sum, out_t * shrink + more_out

    far = ROW * pair

    @pl.when(my_core == 0)
    def _():
        for core in range(CORES):
            arrived(1, 0, core)

    state = fold_in(far, pair, (row_max, row_sum, out_t))
    gradp[pl.ds(far, pair), :] = grad_probs_of(pl.ds(far, pair))
    def hear(*places):
        for place in places:
            for core in range(CORES):
                arrived(1, place, core)

        @pl.when(my_core == 1)
        def _():
            for place in places:
                for core in range(CORES):
                    to_sibling(place, core)

    hear(1, 3)
    state = fold_in(far + pair, 2 * pair, state)
    hear(2)
    row_max, row_sum, out_t = fold_in(far + 3 * pair, pair, state)

    inverse = jnp.where(rows_left > 0, 1.0 / row_sum, 0.0)
    out_t = (out_t * inverse).astype(BF16)
    row_dot = jnp.sum(grad_t * out_t.astype(F32), axis=0, keepdims=True)
    factors = [jnp.exp2(past - row_max) * inverse for past in phase_max]

    def back(at, cols, grad_probs, factor):
        probs = weight[at, cols].astype(F32) * factor[:, cols]
        grad_logits = (probs * (grad_probs - row_dot[:, cols])).astype(BF16)
        weight[at, cols] = grad_logits
        grad_vals = dot(probs.astype(BF16), grads[cols, :], 1, 0)
        grad_keys = dot(grad_logits, queries[cols, :], 1, 0) * SCALE
        return grad_keys, grad_vals

    def term_copy(source, target, sent, landed, to):
        return pltpu.make_async_remote_copy(
            src_ref=source,
            dst_ref=target,
            send_sem=sum_send_sem.at[sent],
            recv_sem=sum_recv_sem.at[landed],
            device_id={"roll": device(*to)},
            device_id_type=MESH,
        )

    def ship(source, target, index, to):
        copy = term_copy(source, target, index, index, to)
        copy.start()
        return copy

    sums = {}

    def prefix_back(first, count, grad_probs, factor):
        grad_keys, grad_vals = back(pl.ds(first, count), all_cols, grad_probs, factor)
        for index, (half, place, core) in enumerate(blocks_in(first, count)):
            at = half * ROW + POS[place]
            rows = slice(index * BLOCK, (index + 1) * BLOCK)
            if core == 0:
                own_sum[at, :, 0:HD] = grad_keys[rows]
                own_sum[at, :, HD : 2 * HD] = grad_vals[rows]
            else:
                to_core[at, :, 0:HD] = grad_keys[rows].astype(BF16)
                to_core[at, :, HD : 2 * HD] = grad_vals[rows].astype(BF16)
                sums["core", at] = ship(to_core.at[at], from_core.at[at], at, (0, 0, 1))

    def chip_total(at):
        sums["core", at].wait_recv()
        return own_sum[at] + from_core[at].astype(F32)

    def send_on(half, place, to):
        at = half * ROW + POS[place]
        to_owner[at] = chip_total(at).astype(BF16)
        lands = half * ROW + POS[(ROW - place) % ROW]
        sums["owner", lands] = ship(
            to_owner.at[at], from_owner.at[lands], HALVES * ROW + lands, to
        )

    def neighbour_copy(place):
        at = ROW + POS[place]
        first = (POS[ROW - place] - 1) * CORES
        return term_copy(
            to_owner.at[at],
            from_row.at[first + my_core],
            2 * HALVES * ROW + place,
            2 * HALVES * ROW + first + my_core,
            (0, place, speaker),
        )

    def neighbour_arrived(index):
        term_copy(
            from_row.at[index], from_row.at[index], 0, 2 * HALVES * ROW + index, (0, 0, 1)
        ).wait_recv()

    sibling_copy = term_copy(to_owner.at[ROW], from_row.at[4], 20, 20, (0, 0, 1))

    def opposite_copy(core):
        return term_copy(
            to_opposite.at[core],
            from_owner.at[ROW],
            21 + core,
            HALVES * ROW + ROW,
            (1, 0, (core + 1) % CORES),
        )

    last = pl.ds(far + 3 * pair, pair)
    cross = pl.ds(far + 2 * pair, pair)
    straight = pl.ds(far + pair, pair)
    prefix_back(far + 2 * pair, pair, grad_probs_of(cross), factors[2])
    prefix_back(far + 3 * pair, pair, grad_probs_of(last), factors[3])
    prefix_back(far + pair, pair, grad_probs_of(straight), factors[2])
    for place in (1, 3):
        at = ROW + POS[place]
        to_owner[at] = chip_total(at).astype(BF16)
        neighbour_copy(place).start()
    send_on(1, 2, (1, 2, 0))
    prefix_back(far, pair, gradp[pl.ds(far, pair), :], factors[1])
    prefix_back(2 * pair, 2 * pair, gradp[pl.ds(2 * pair, 2 * pair), :], factors[0])

    @pl.when(my_core == 0)
    def _():
        to_owner[ROW] = chip_total(ROW).astype(BF16)
        sibling_copy.start()

    prefix_back(0, 2 * pair, gradp[pl.ds(0, 2 * pair), :], factors[0])
    send_on(0, 2, (0, 2, 0))
    send_on(0, 3, (0, 3, 0))
    send_on(0, 1, (0, 1, 0))
    grad_keys, grad_vals = back(
        own_rows, own_cols, gradp[own_rows, own_cols], factors[0]
    )
    roll_dkv[0, :, 0:HD] = grad_keys.astype(BF16)
    roll_dkv[0, :, HD : 2 * HD] = grad_vals.astype(BF16)

    @pl.when(my_core == 1)
    def _():
        term = chip_total(ROW)
        for index in (1, 3):
            neighbour_arrived(index)
            term = term + from_row[index].astype(F32)
        to_opposite[1] = term.astype(BF16)
        opposite_copy(1).start()
        sibling_copy.wait_recv()
        term = from_row[4].astype(F32)
        for index in (0, 2):
            neighbour_arrived(index)
            term = term + from_row[index].astype(F32)
        to_opposite[0] = term.astype(BF16)
        opposite_copy(0).start()

    out = out_t.T
    for head in range(HEADS):
        columns = slice(head * HD, (head + 1) * HD)
        roll_out[0, :, columns] = out[head * RESP : (head + 1) * RESP]
        at = ROLL_ROWS + head * BLOCK
        pre_out[:, columns] = out[at : at + BLOCK]
    keys_t[:, 0:PREFIX] = kvs[:, 0:HD].T
    keys_t[:, own_rows] = rkv[:, 0:HD].T
    grad_query = dot(keys_t[:, 0:PREFIX], weight[0:PREFIX, :], 1, 0)
    grad_query = widen(
        grad_query, dot(keys_t[:, own_rows], weight[own_rows, own_cols], 1, 0), jnp.add
    )
    grad_query = (grad_query * SCALE).astype(BF16).T
    for head in range(HEADS):
        columns = slice(head * HD, (head + 1) * HD)
        roll_dq[0, :, columns] = grad_query[head * RESP : (head + 1) * RESP]
        at = ROLL_ROWS + head * BLOCK
        pre_dq[:, columns] = grad_query[at : at + BLOCK]

    total = chip_total(0)
    for at in (1, 2, 3, ROW + POS[2]):
        sums["owner", at].wait_recv()
        total = total + from_owner[at].astype(F32)
    opposite_copy(0).wait_recv()
    pre_dkv[...] = (total + from_owner[ROW].astype(F32)).astype(BF16)
    for copy in (*copies, *sums.values(), neighbour_copy(1), neighbour_copy(3)):
        copy.wait_send()

    @pl.when(my_core == 0)
    def _():
        sibling_copy.wait_send()

    @pl.when(my_core == 1)
    def _():
        for core in range(CORES):
            opposite_copy(core).wait_send()
            for place in (1, 2, 3):
                along_row(place, core, start=False)
            for place in range(ROW):
                to_sibling(place, core, start=False)


def drain(*refs):
    count = (len(refs) - 1) // 2
    sem = refs[-1]
    copies = [
        pltpu.make_async_copy(refs[index], refs[count + index], sem.at[index])
        for index in range(count)
    ]
    for copy in copies:
        copy.start()
    for copy in copies:
        copy.wait()


def on_device(pre_q, pre_kv, roll_q, roll_kv, pre_grad, roll_grad, pre_len, roll_len):
    smem = pl.BlockSpec(memory_space=pltpu.SMEM)
    vmem = pl.BlockSpec(memory_space=pltpu.VMEM)
    anywhere = pl.BlockSpec(memory_space=pl.ANY)
    like = lambda array: pltpu.VMEM(array.shape, BF16)
    final = lambda array: jax.ShapeDtypeStruct(array.shape, BF16)
    copies = 2 * GROUP
    sums = 24
    results = pl.pallas_call(
        kernel,
        out_shape=(
            like(pre_q),
            like(roll_q),
            like(pre_q),
            like(roll_q),
            like(pre_kv),
            like(roll_kv),
        ),
        in_specs=[smem] * 2 + [anywhere] * 6,
        out_specs=[vmem] * 6,
        scratch_shapes=[
            pltpu.VMEM((RESP, HEADS * HD), BF16),
            pltpu.VMEM((RESP, HEADS * HD), BF16),
            pltpu.VMEM((BLOCK, HEADS * HD), BF16),
            pltpu.VMEM((BLOCK, HEADS * HD), BF16),
            pltpu.VMEM((RESP, 2 * HD), BF16),
            pltpu.VMEM((PREFIX, 2 * HD), BF16),
            pltpu.VMEM((ROWS, HD), BF16),
            pltpu.VMEM((ROWS, HD), BF16),
            pltpu.VMEM((PREFIX + RESP, ROWS), F32),
            pltpu.VMEM((PREFIX + RESP, ROWS), BF16),
            pltpu.VMEM((PREFIX + RESP, ROWS), F32),
            pltpu.VMEM((HD, PREFIX + RESP), BF16),
            pltpu.VMEM((HD, PREFIX + RESP), BF16),
            pltpu.VMEM((HALVES * ROW, BLOCK, 2 * HD), BF16),
            pltpu.VMEM((HALVES * ROW, BLOCK, 2 * HD), BF16),
            pltpu.VMEM((HALVES * ROW, BLOCK, 2 * HD), F32),
            pltpu.VMEM((HALVES * ROW, BLOCK, 2 * HD), BF16),
            pltpu.VMEM((HALVES * ROW, BLOCK, 2 * HD), BF16),
            pltpu.VMEM((5, BLOCK, 2 * HD), BF16),
            pltpu.VMEM((CORES, BLOCK, 2 * HD), BF16),
            pltpu.SemaphoreType.DMA((6,)),
            pltpu.SemaphoreType.DMA((copies,)),
            pltpu.SemaphoreType.DMA((copies,)),
            pltpu.SemaphoreType.DMA((sums,)),
            pltpu.SemaphoreType.DMA((sums,)),
        ],
        compiler_params=pltpu.CompilerParams(
            collective_id=0, has_side_effects=True, vmem_limit_bytes=56 << 20
        ),
    )(pre_len, roll_len, pre_q, pre_kv, roll_q, roll_kv, pre_grad, roll_grad)
    return pl.pallas_call(
        drain,
        out_shape=tuple(final(array) for array in (pre_q, roll_q, pre_q, roll_q, pre_kv, roll_kv)),
        in_specs=[vmem] * 6,
        out_specs=[anywhere] * 6,
        scratch_shapes=[pltpu.SemaphoreType.DMA((6,))],
    )(*(pltpu.with_memory_space_constraint(result, pltpu.VMEM) for result in results))


def solution(mesh):
    in_specs = (
        P(("prompt", "roll"), None),
        P(("prompt", "roll"), None),
        P(("prompt", "roll"), None, None),
        P(("prompt", "roll"), None, None),
        P(("prompt", "roll"), None),
        P(("prompt", "roll"), None, None),
        P("prompt"),
        P(("prompt", "roll")),
    )
    out_specs = (
        P(("prompt", "roll"), None),
        P(("prompt", "roll"), None, None),
        P(("prompt", "roll"), None),
        P(("prompt", "roll"), None, None),
        P(("prompt", "roll"), None),
        P(("prompt", "roll"), None, None),
    )
    return jax.shard_map(
        on_device, mesh=mesh, in_specs=in_specs, out_specs=out_specs, check_vma=False
    )
```

```python
import functools

import jax
import jax.numpy as jnp
from jax import lax
from jax.experimental import pallas as pl
from jax.experimental.pallas import tpu as pltpu
from jax.sharding import PartitionSpec as P

F32 = jnp.float32
BF16 = jnp.bfloat16
MESH = pl.DeviceIdType.MESH
masked_score = -1e30
HALVES, ROW, CORES = 2, 4, 2
BLOCK = 64
RESP = 128
HEADS = 8
HD = 128
GROUP = HALVES * ROW * CORES
PREFIX = GROUP * BLOCK
ROLL_ROWS = HEADS * RESP
ROWS = HEADS * (RESP + BLOCK)
SCALE = HD**-0.5
LOG2E = 1.4426950408889634


def dot(left, right, left_dim, right_dim):
    return lax.dot_general(
        left, right, (((left_dim,), (right_dim,)), ((), ())), preferred_element_type=F32
    )


POS = (0, 1, 3, 2)
LAYOUT = ((0, 0), (0, 1), (1, 0), (3, 0), (1, 1), (3, 1), (2, 0), (2, 1))


def slot(half, place, core):
    return half * len(LAYOUT) + LAYOUT.index((place, core))


def blocks_in(first, count):
    slots = range(first // BLOCK, (first + count) // BLOCK)
    return [(at // len(LAYOUT), *LAYOUT[at % len(LAYOUT)]) for at in slots]


def rows_of(half, place, core):
    return pl.ds(slot(half, place, core) * BLOCK, BLOCK)


def fold8(values, combine):
    return combine(values.reshape(values.shape[0] // 8, 8, values.shape[1]), axis=0)


def kernel(
    pre_len_ref,
    roll_len_ref,
    pre_q,
    pre_kv,
    roll_q,
    roll_kv,
    pre_grad,
    roll_grad,
    pre_out,
    roll_out,
    pre_dq,
    roll_dq,
    pre_dkv,
    roll_dkv,
    rq,
    rg,
    pq,
    pg,
    rkv,
    kvs,
    queries,
    grads,
    score,
    weight,
    gradp,
    keys_t,
    vals_t,
    to_core,
    from_core,
    own_sum,
    to_owner,
    from_owner,
    from_row,
    to_opposite,
    load_sem,
    send_sem,
    recv_sem,
    sum_send_sem,
    sum_recv_sem,
):
    me = lax.axis_index("roll")
    my_half, my_place, my_core = me // (ROW * CORES), (me // CORES) % ROW, me % CORES

    def device(half, place, core):
        return (
            ((my_half + half) % HALVES) * (ROW * CORES)
            + ((my_place + place) % ROW) * CORES
            + (my_core + core) % CORES
        )

    speaker = 1 - my_core
    partners = [(0, 0, 1), (0, 1, 0), (0, 3, 0), (0, 2, 0)]
    barrier = pltpu.get_barrier_semaphore()

    def announce(partner):
        pl.semaphore_signal(
            barrier, inc=1, device_id={"roll": device(*partner)}, device_id_type=MESH
        )

    @pl.when(my_core == 1)
    def _():
        announce((1, 0, 0))
        announce((1, 0, 1))

    for partner in partners:
        announce(partner)

    loads = []
    for index, (source, target) in enumerate(
        (
            (pre_kv, kvs.at[rows_of(0, 0, 0)]),
            (roll_kv.at[0], rkv),
            (roll_q.at[0], rq),
            (pre_q, pq),
            (roll_grad.at[0], rg),
            (pre_grad, pg),
        )
    ):
        loads.append(pltpu.make_async_copy(source, target, load_sem.at[index]))
        loads[-1].start()

    def block_copy(source, at, index, to):
        return pltpu.make_async_remote_copy(
            src_ref=source,
            dst_ref=kvs.at[pl.ds(at * BLOCK, BLOCK)],
            send_sem=send_sem.at[index],
            recv_sem=recv_sem.at[at],
            device_id={"roll": device(*to)},
            device_id_type=MESH,
        )

    def push(source, at, index, to):
        copy = block_copy(source, at, index, to)
        copy.start()
        return copy

    def arrived(*block):
        at = slot(*block)
        block_copy(kvs.at[rows_of(*block)], at, 0, (0, 0, 1)).wait_recv()

    def relay_near(place):
        at = slot(0, place, 1)
        copies.append(push(kvs.at[rows_of(0, place, 0)], at, at, (0, 0, 1)))

    def to_sibling(place, core, start=True):
        at = slot(1, place, 1 - core)
        copy = block_copy(kvs.at[rows_of(1, place, core)], at, GROUP + at, (0, 0, 1))
        copy.start() if start else copy.wait_send()

    def along_row(place, core, start=True):
        at = slot(1, ROW - place, core)
        copy = block_copy(kvs.at[rows_of(1, 0, core)], at, GROUP + place * CORES + core, (0, place, 0))
        copy.start() if start else copy.wait_send()

    copies = []
    loads[0].wait()
    pl.semaphore_wait(barrier, len(partners) + 1)
    held = kvs.at[rows_of(0, 0, 0)]
    copies.append(push(held, slot(1, 0, 0) + speaker, 0, (1, 0, speaker)))
    for place in (2, 1, 3):
        at = slot(0, ROW - place, 0)
        copies.append(push(held, at, at, (0, place, 0)))
    at = slot(0, 0, 1)
    copies.append(push(held, at, at, (0, 0, 1)))

    pre_len = pre_len_ref[0]
    roll_len = roll_len_ref[0]
    lane = lax.broadcasted_iota(jnp.int32, (1, ROWS), 1)
    is_roll = lane < ROLL_ROWS
    query_pos = me * BLOCK + lane % BLOCK
    limit = jnp.where(is_roll, pre_len - 1, jnp.minimum(query_pos, pre_len - 1))
    own_limit = jnp.minimum(lane[:, :ROLL_ROWS] % RESP, roll_len - 1)
    rows_left = jnp.where(is_roll, roll_len - lane % RESP, pre_len - query_pos)

    for load in loads[1:]:
        load.wait()
    for head in range(HEADS):
        columns = slice(head * HD, (head + 1) * HD)
        at = pl.ds(head * RESP, RESP)
        queries[at, :] = rq[:, columns]
        grads[at, :] = rg[:, columns]
        at = pl.ds(ROLL_ROWS + head * BLOCK, BLOCK)
        queries[at, :] = pq[:, columns]
        grads[at, :] = pg[:, columns]

    own_rows = pl.ds(PREFIX, RESP)
    all_cols = slice(0, ROWS)
    own_cols = slice(0, ROLL_ROWS)

    def take(first, count):
        at = pl.ds(first, count)
        vals_t[:, at] = kvs[at, HD : 2 * HD].T
        row = lax.broadcasted_iota(jnp.int32, (count, 1), 0)
        base = 0
        for index, block in enumerate(blocks_in(first, count)):
            base = jnp.where(row // BLOCK == index, device(*block) * BLOCK, base)
        key_pos = base + row % BLOCK
        logits = dot(kvs[at, 0:HD], queries[...], 1, 1) * (SCALE * LOG2E)
        logits = jnp.where(key_pos <= limit, logits, masked_score)
        score[at, :] = logits
        return fold8(logits, jnp.max)

    def widen(total, own, combine):
        return jnp.concatenate([combine(total[:, own_cols], own), total[:, ROLL_ROWS:]], axis=1)

    def weigh(at, cols, row_max):
        expo = jnp.exp2(score[at, cols] - row_max)
        rounded = expo.astype(BF16)
        weight[at, cols] = rounded
        return fold8(expo, jnp.sum), dot(vals_t[:, at], rounded, 1, 0)

    def grad_probs_of(at):
        return dot(kvs[at, HD : 2 * HD], grads[...], 1, 1)

    own_key = lax.broadcasted_iota(jnp.int32, (RESP, 1), 0)
    own_logits = dot(rkv[:, 0:HD], queries[own_cols, :], 1, 1) * (SCALE * LOG2E)
    own_logits = jnp.where(own_key <= own_limit, own_logits, masked_score)
    score[own_rows, own_cols] = own_logits
    own_max = fold8(own_logits, jnp.max)
    vals_t[:, own_rows] = rkv[:, HD : 2 * HD].T
    gradp[own_rows, own_cols] = dot(rkv[:, HD : 2 * HD], grads[own_cols, :], 1, 1)
    grad_t = grads[...].T.astype(F32)

    pair = CORES * BLOCK
    for place in (1, 3, 2):
        arrived(0, place, 0)
        relay_near(place)
    arrived(0, 0, 1)
    near_max = take(0, 2 * pair)

    @pl.when(my_core == 1)
    def _():
        for core in range(CORES):
            arrived(1, 0, core)
        for place in (1, 3):
            for core in range(CORES):
                along_row(place, core)
        for core in range(CORES):
            to_sibling(0, core)
            along_row(2, core)

    for place in (1, 3, 2):
        arrived(0, place, 1)
    near_max = jnp.maximum(near_max, take(2 * pair, 2 * pair))
    near_max = widen(near_max, own_max, jnp.maximum)
    row_max = jnp.max(near_max, axis=0, keepdims=True)
    near = pl.ds(0, ROW * pair)
    row_sum, out_t = weigh(near, all_cols, row_max)
    own_sum_8, own_out = weigh(own_rows, own_cols, row_max[:, own_cols])
    row_sum = jnp.sum(widen(row_sum, own_sum_8, jnp.add), axis=0, keepdims=True)
    out_t = widen(out_t, own_out, jnp.add)
    phase_max = [row_max]
    gradp[near, :] = grad_probs_of(near)

    def fold_in(first, count, state):
        row_max, row_sum, out_t = state
        new_max = jnp.max(take(first, count), axis=0, keepdims=True)
        new_max = jnp.maximum(row_max, new_max)
        shrink = jnp.exp2(row_max - new_max)
        more_sum, more_out = weigh(pl.ds(first, count), all_cols, new_max)
        phase_max.append(new_max)
        row_sum = row_sum * shrink + jnp.sum(more_sum, axis=0, keepdims=True)
        return new_max, row_sum, out_t * shrink + more_out

    far = ROW * pair

    @pl.when(my_core == 0)
    def _():
        for core in range(CORES):
            arrived(1, 0, core)

    state = fold_in(far, pair, (row_max, row_sum, out_t))
    gradp[pl.ds(far, pair), :] = grad_probs_of(pl.ds(far, pair))
    def hear(*places):
        for place in places:
            for core in range(CORES):
                arrived(1, place, core)

        @pl.when(my_core == 1)
        def _():
            for place in places:
                for core in range(CORES):
                    to_sibling(place, core)

    hear(1, 3)
    state = fold_in(far + pair, 2 * pair, state)
    hear(2)
    row_max, row_sum, out_t = fold_in(far + 3 * pair, pair, state)

    inverse = jnp.where(rows_left > 0, 1.0 / row_sum, 0.0)
    out_t = (out_t * inverse).astype(BF16)
    row_dot = jnp.sum(grad_t * out_t.astype(F32), axis=0, keepdims=True)
    factors = [jnp.exp2(past - row_max) * inverse for past in phase_max]

    def back(at, cols, grad_probs, factor):
        probs = weight[at, cols].astype(F32) * factor[:, cols]
        grad_logits = (probs * (grad_probs - row_dot[:, cols])).astype(BF16)
        weight[at, cols] = grad_logits
        grad_vals = dot(probs.astype(BF16), grads[cols, :], 1, 0)
        grad_keys = dot(grad_logits, queries[cols, :], 1, 0) * SCALE
        return grad_keys, grad_vals

    def term_copy(source, target, sent, landed, to):
        return pltpu.make_async_remote_copy(
            src_ref=source,
            dst_ref=target,
            send_sem=sum_send_sem.at[sent],
            recv_sem=sum_recv_sem.at[landed],
            device_id={"roll": device(*to)},
            device_id_type=MESH,
        )

    def ship(source, target, index, to):
        copy = term_copy(source, target, index, index, to)
        copy.start()
        return copy

    sums = {}

    def prefix_back(first, count, grad_probs, factor):
        grad_keys, grad_vals = back(pl.ds(first, count), all_cols, grad_probs, factor)
        for index, (half, place, core) in enumerate(blocks_in(first, count)):
            at = half * ROW + POS[place]
            rows = slice(index * BLOCK, (index + 1) * BLOCK)
            if core == 0:
                own_sum[at, :, 0:HD] = grad_keys[rows]
                own_sum[at, :, HD : 2 * HD] = grad_vals[rows]
            else:
                to_core[at, :, 0:HD] = grad_keys[rows].astype(BF16)
                to_core[at, :, HD : 2 * HD] = grad_vals[rows].astype(BF16)
                sums["core", at] = ship(to_core.at[at], from_core.at[at], at, (0, 0, 1))

    def chip_total(at):
        sums["core", at].wait_recv()
        return own_sum[at] + from_core[at].astype(F32)

    def send_on(half, place, to):
        at = half * ROW + POS[place]
        to_owner[at] = chip_total(at).astype(BF16)
        lands = half * ROW + POS[(ROW - place) % ROW]
        sums["owner", lands] = ship(
            to_owner.at[at], from_owner.at[lands], HALVES * ROW + lands, to
        )

    def neighbour_copy(place):
        at = ROW + POS[place]
        first = (POS[ROW - place] - 1) * CORES
        return term_copy(
            to_owner.at[at],
            from_row.at[first + my_core],
            2 * HALVES * ROW + place,
            2 * HALVES * ROW + first + my_core,
            (0, place, speaker),
        )

    def neighbour_arrived(index):
        term_copy(
            from_row.at[index], from_row.at[index], 0, 2 * HALVES * ROW + index, (0, 0, 1)
        ).wait_recv()

    sibling_copy = term_copy(to_owner.at[ROW], from_row.at[4], 20, 20, (0, 0, 1))

    def opposite_copy(core):
        return term_copy(
            to_opposite.at[core],
            from_owner.at[ROW],
            21 + core,
            HALVES * ROW + ROW,
            (1, 0, (core + 1) % CORES),
        )

    last = pl.ds(far + 3 * pair, pair)
    cross = pl.ds(far + 2 * pair, pair)
    straight = pl.ds(far + pair, pair)
    prefix_back(far + 2 * pair, pair, grad_probs_of(cross), factors[2])
    prefix_back(far + 3 * pair, pair, grad_probs_of(last), factors[3])
    prefix_back(far + pair, pair, grad_probs_of(straight), factors[2])
    for place in (1, 3):
        at = ROW + POS[place]
        to_owner[at] = chip_total(at).astype(BF16)
        neighbour_copy(place).start()
    send_on(1, 2, (1, 2, 0))
    prefix_back(far, pair, gradp[pl.ds(far, pair), :], factors[1])
    prefix_back(2 * pair, 2 * pair, gradp[pl.ds(2 * pair, 2 * pair), :], factors[0])

    @pl.when(my_core == 0)
    def _():
        to_owner[ROW] = chip_total(ROW).astype(BF16)
        sibling_copy.start()

    prefix_back(0, 2 * pair, gradp[pl.ds(0, 2 * pair), :], factors[0])
    send_on(0, 2, (0, 2, 0))
    send_on(0, 3, (0, 3, 0))
    send_on(0, 1, (0, 1, 0))
    grad_keys, grad_vals = back(
        own_rows, own_cols, gradp[own_rows, own_cols], factors[0]
    )
    roll_dkv[0, :, 0:HD] = grad_keys.astype(BF16)
    roll_dkv[0, :, HD : 2 * HD] = grad_vals.astype(BF16)

    @pl.when(my_core == 1)
    def _():
        term = chip_total(ROW)
        for index in (1, 3):
            neighbour_arrived(index)
            term = term + from_row[index].astype(F32)
        to_opposite[1] = term.astype(BF16)
        opposite_copy(1).start()
        sibling_copy.wait_recv()
        term = from_row[4].astype(F32)
        for index in (0, 2):
            neighbour_arrived(index)
            term = term + from_row[index].astype(F32)
        to_opposite[0] = term.astype(BF16)
        opposite_copy(0).start()

    out = out_t.T
    for head in range(HEADS):
        columns = slice(head * HD, (head + 1) * HD)
        roll_out[0, :, columns] = out[head * RESP : (head + 1) * RESP]
        at = ROLL_ROWS + head * BLOCK
        pre_out[:, columns] = out[at : at + BLOCK]
    keys_t[:, 0:PREFIX] = kvs[:, 0:HD].T
    keys_t[:, own_rows] = rkv[:, 0:HD].T
    grad_query = dot(keys_t[:, 0:PREFIX], weight[0:PREFIX, :], 1, 0)
    grad_query = widen(
        grad_query, dot(keys_t[:, own_rows], weight[own_rows, own_cols], 1, 0), jnp.add
    )
    grad_query = (grad_query * SCALE).astype(BF16).T
    for head in range(HEADS):
        columns = slice(head * HD, (head + 1) * HD)
        roll_dq[0, :, columns] = grad_query[head * RESP : (head + 1) * RESP]
        at = ROLL_ROWS + head * BLOCK
        pre_dq[:, columns] = grad_query[at : at + BLOCK]

    total = chip_total(0)
    for at in (1, 2, 3, ROW + POS[2]):
        sums["owner", at].wait_recv()
        total = total + from_owner[at].astype(F32)
    opposite_copy(0).wait_recv()
    pre_dkv[...] = (total + from_owner[ROW].astype(F32)).astype(BF16)
    for copy in (*copies, *sums.values(), neighbour_copy(1), neighbour_copy(3)):
        copy.wait_send()

    @pl.when(my_core == 0)
    def _():
        sibling_copy.wait_send()

    @pl.when(my_core == 1)
    def _():
        for core in range(CORES):
            opposite_copy(core).wait_send()
            for place in (1, 2, 3):
                along_row(place, core, start=False)
            for place in range(ROW):
                to_sibling(place, core, start=False)


def drain(*refs):
    count = (len(refs) - 1) // 2
    sem = refs[-1]
    copies = [
        pltpu.make_async_copy(refs[index], refs[count + index], sem.at[index])
        for index in range(count)
    ]
    for copy in copies:
        copy.start()
    for copy in copies:
        copy.wait()


def on_device(pre_q, pre_kv, roll_q, roll_kv, pre_grad, roll_grad, pre_len, roll_len):
    smem = pl.BlockSpec(memory_space=pltpu.SMEM)
    vmem = pl.BlockSpec(memory_space=pltpu.VMEM)
    anywhere = pl.BlockSpec(memory_space=pl.ANY)
    like = lambda array: pltpu.VMEM(array.shape, BF16)
    final = lambda array: jax.ShapeDtypeStruct(array.shape, BF16)
    copies = 2 * GROUP
    sums = 24
    results = pl.pallas_call(
        kernel,
        out_shape=(
            like(pre_q),
            like(roll_q),
            like(pre_q),
            like(roll_q),
            like(pre_kv),
            like(roll_kv),
        ),
        in_specs=[smem] * 2 + [anywhere] * 6,
        out_specs=[vmem] * 6,
        scratch_shapes=[
            pltpu.VMEM((RESP, HEADS * HD), BF16),
            pltpu.VMEM((RESP, HEADS * HD), BF16),
            pltpu.VMEM((BLOCK, HEADS * HD), BF16),
            pltpu.VMEM((BLOCK, HEADS * HD), BF16),
            pltpu.VMEM((RESP, 2 * HD), BF16),
            pltpu.VMEM((PREFIX, 2 * HD), BF16),
            pltpu.VMEM((ROWS, HD), BF16),
            pltpu.VMEM((ROWS, HD), BF16),
            pltpu.VMEM((PREFIX + RESP, ROWS), F32),
            pltpu.VMEM((PREFIX + RESP, ROWS), BF16),
            pltpu.VMEM((PREFIX + RESP, ROWS), F32),
            pltpu.VMEM((HD, PREFIX + RESP), BF16),
            pltpu.VMEM((HD, PREFIX + RESP), BF16),
            pltpu.VMEM((HALVES * ROW, BLOCK, 2 * HD), BF16),
            pltpu.VMEM((HALVES * ROW, BLOCK, 2 * HD), BF16),
            pltpu.VMEM((HALVES * ROW, BLOCK, 2 * HD), F32),
            pltpu.VMEM((HALVES * ROW, BLOCK, 2 * HD), BF16),
            pltpu.VMEM((HALVES * ROW, BLOCK, 2 * HD), BF16),
            pltpu.VMEM((5, BLOCK, 2 * HD), BF16),
            pltpu.VMEM((CORES, BLOCK, 2 * HD), BF16),
            pltpu.SemaphoreType.DMA((6,)),
            pltpu.SemaphoreType.DMA((copies,)),
            pltpu.SemaphoreType.DMA((copies,)),
            pltpu.SemaphoreType.DMA((sums,)),
            pltpu.SemaphoreType.DMA((sums,)),
        ],
        compiler_params=pltpu.CompilerParams(
            collective_id=0, has_side_effects=True, vmem_limit_bytes=56 << 20
        ),
    )(pre_len, roll_len, pre_q, pre_kv, roll_q, roll_kv, pre_grad, roll_grad)
    return pl.pallas_call(
        drain,
        out_shape=tuple(final(array) for array in (pre_q, roll_q, pre_q, roll_q, pre_kv, roll_kv)),
        in_specs=[vmem] * 6,
        out_specs=[anywhere] * 6,
        scratch_shapes=[pltpu.SemaphoreType.DMA((6,))],
    )(*(pltpu.with_memory_space_constraint(result, pltpu.VMEM) for result in results))


def solution(mesh):
    in_specs = (
        P(("prompt", "roll"), None),
        P(("prompt", "roll"), None),
        P(("prompt", "roll"), None, None),
        P(("prompt", "roll"), None, None),
        P(("prompt", "roll"), None),
        P(("prompt", "roll"), None, None),
        P("prompt"),
        P(("prompt", "roll")),
    )
    out_specs = (
        P(("prompt", "roll"), None),
        P(("prompt", "roll"), None, None),
        P(("prompt", "roll"), None),
        P(("prompt", "roll"), None, None),
        P(("prompt", "roll"), None),
        P(("prompt", "roll"), None, None),
    )
    return jax.shard_map(
        on_device, mesh=mesh, in_specs=in_specs, out_specs=out_specs, check_vma=False
    )
```
